1024 devices in a mesh: row: 32 (over z, x_hi), col: 32 (over y, x_lo, core).
Axes of the slice: x: 4 (x_hi: 2, x_lo: 2; x = x_hi * 2 + x_lo), y: 8, z: 16, core: 2. Of those that a mesh axis runs over, the one named last changes fastest.
Arguments:
- a_vals: float32 [32, 64, 92, 92], P('row', 'col'), may hold values from -0.625 to 0.625
- a_row: int32 [32, 64], P('row', 'col'), may hold values from 0 to 1, as said below
- a_col: int32 [32, 64], P('row', 'col'), may hold values from 0 to 63, as said below
- a_count: int32 [32, 32], P('row', 'col'), may hold values from 0 to 2, as said below
- b_vals: float32 [32, 64, 92, 92], P('row', 'col'), may hold values from -2 to 2
- b_rows: int32 [32, 64], P('row', 'col'), may hold values from 0 to 63, as said below
- c_keep: int32 [64, 64], P('row', 'col'), may hold values 0 or 1
Outputs:
- c_kept: float32 [64, 64, 92, 92], P('row', 'col')
The draws below stay inside these ranges and needn't reach their ends.
Inputs may be any that keep to these rules, and one draw needn't show every extreme that they name: `a_count`: in every grid row the counts sum to 32, and at least one device holds 2. `a_row`: the live slots of one grid row list each nonzero block of its 2 block rows exactly once; dead slots hold arbitrary values. `a_col`: each block row of the left factor has exactly 16 nonzero blocks, at distinct block columns. `b_rows`: distinct within each block column.
All inputs are finite; a program needn't handle non-finite values. No bound on the sum of `c_keep` on one device may be relied on, other than what follows from the above.
Results may differ from the reference program's by a relative error of at most 0.0003.
Values sent between devices are 32-bit elements; how exact they have to be, the bound alone decides.
No kernel may reach another device: no remote copies, remote signals or barrier semaphores. Data moves between devices by JAX's collectives and lax.ppermute only.
A program may use at most 64 MiB of HBM per device.

```python
import jax
import jax.numpy as jnp
from jax import lax

BLK = 92
KA = 16
NBLK = 64
BR = 2
KB = 32
CAPA = 2
N_ROW = 32
N_COL = 32


def slab_lists(key):
    blocks_total = BR * KA

    def one_grid_row(row_key):
        key_cols, key_order, key_full, key_score, key_pad = jax.random.split(row_key, 5)
        column_keys = jax.random.split(key_cols, BR)
        columns = jax.vmap(lambda sub_key: jax.random.permutation(sub_key, NBLK)[:KA])(column_keys)
        local_rows = jnp.broadcast_to(jnp.arange(BR, dtype=jnp.int32)[:, None], (BR, KA)).reshape(-1)
        shuffle = jax.random.permutation(key_order, blocks_total)
        list_rows = local_rows[shuffle]
        list_cols = columns.reshape(-1).astype(jnp.int32)[shuffle]
        full_device = jax.random.randint(key_full, (), 0, N_COL)
        scores = jax.random.permutation(key_score, N_COL * CAPA).reshape(N_COL, CAPA).astype(jnp.int32)
        scores = jnp.where(jnp.arange(N_COL)[:, None] == full_device, scores + N_COL * CAPA, scores)
        ordered = jnp.sort(scores.reshape(-1))
        cutoff = ordered[N_COL * CAPA - blocks_total]
        chosen = (scores >= cutoff).astype(jnp.int32)
        counts = jnp.sum(chosen, axis=1).astype(jnp.int32)
        starts = jnp.cumsum(counts) - counts
        slots = jnp.arange(CAPA, dtype=jnp.int32)
        live_slot = slots[None, :] < counts[:, None]
        ranks = jnp.clip(starts[:, None] + slots[None, :], 0, blocks_total - 1)
        pad_rows = jax.random.randint(key_pad, (N_COL, CAPA), 0, BR)
        pad_cols = jax.random.randint(jax.random.fold_in(key_pad, 1), (N_COL, CAPA), 0, NBLK)
        rows_out = jnp.where(live_slot, list_rows[ranks], pad_rows).reshape(-1)
        cols_out = jnp.where(live_slot, list_cols[ranks], pad_cols).reshape(-1)
        return (counts, rows_out, cols_out)
    return jax.vmap(one_grid_row)(jax.random.split(key, N_ROW))


def draw_a_count(key, part):
    shared = slab_lists(key)
    return shared[0].astype(jnp.int32)


def draw_a_row(key, part):
    shared = slab_lists(key)
    return shared[1].astype(jnp.int32)


def draw_a_col(key, part):
    shared = slab_lists(key)
    return shared[2].astype(jnp.int32)


def draw_b_rows(key, part):
    key = jax.random.fold_in(key, 7)
    column_keys = jax.random.split(key, NBLK)
    chosen_rows = jax.vmap(lambda sub_key: jax.random.permutation(sub_key, NBLK)[:KB])(column_keys)
    return chosen_rows.T.astype(jnp.int32)


def touch_ends(values, key, low, top_value):
    extent = values.shape
    spot = [jax.random.randint(jax.random.fold_in(key, axis), (), 0, extent[axis]) for axis in range(len(extent))]
    values = values.at[tuple(spot)].set(low)
    longest = extent.index(max(extent))
    spot[longest] = (spot[longest] + 1) % extent[longest]
    return values.at[tuple(spot)].set(top_value)


def block_scale(rng, shape, cuts, least, high):
    loudness, own = 1.0, jax.random.fold_in(rng, 6)
    for position, parts in cuts:
        steps = jnp.exp(jax.random.uniform(jax.random.fold_in(own, position), (parts,), jnp.float32, least / len(cuts), high / len(cuts)))
        loudness = loudness * jnp.repeat(steps, shape[position] // parts).reshape([-1 if axis == position else 1 for axis in range(len(shape))])
    return loudness


def bell_draw(stream_key, dims, width, reach, cuts=(), kind=jnp.bfloat16):
    result = jax.random.normal(stream_key, dims, jnp.float32) * width
    if len(cuts) > 0:
        result = block_scale(stream_key, dims, cuts, -0.22, 0.18) * result
    return jnp.clip(result, min=-reach, max=reach).astype(kind)


def setup_inputs(seed: int = 0) -> dict:
    streams_of = jax.random.split(jax.random.key(seed), 8)
    a_vals = bell_draw(streams_of[0], (N_ROW, N_COL * CAPA, BLK, BLK), BLK ** -0.5, 0.625, ((0, 32), (1, 32)), jnp.float32)
    a_row = draw_a_row(jax.random.fold_in(streams_of[7], 71), 0)
    a_col = draw_a_col(jax.random.fold_in(streams_of[7], 71), 0)
    a_count = draw_a_count(jax.random.fold_in(streams_of[7], 71), 0)
    b_vals = bell_draw(streams_of[4], (KB, NBLK, BLK, BLK), (max(1, KA * KB // NBLK)) ** -0.5, 2.0, ((0, 32), (1, 32)), jnp.float32)
    b_rows = draw_b_rows(jax.random.fold_in(streams_of[7], 71), 0)
    c_keep = touch_ends((jax.random.randint(streams_of[6], (NBLK, NBLK), 0, 4) < 3).astype(jnp.int32), jax.random.fold_in(streams_of[6], 1), 0, 1)
    return dict(a_vals=a_vals, a_row=a_row, a_col=a_col, a_count=a_count, b_vals=b_vals, b_rows=b_rows, c_keep=c_keep)


def reference(a_vals, a_row, a_col, a_count, b_vals, b_rows, c_keep):
    highest = lax.Precision.HIGHEST
    b_dense = jnp.zeros((NBLK, NBLK, BLK, BLK), jnp.float32)
    b_dense = b_dense.at[b_rows, jnp.arange(NBLK, dtype=jnp.int32)[None, :]].set(b_vals)
    slot_place = (jnp.arange(N_COL * CAPA, dtype=jnp.int32) % CAPA)[None, :]
    live_slots = slot_place < jnp.repeat(a_count, CAPA, axis=1)

    def grid_row(inputs):
        values, local_rows, columns, alive_mask = inputs
        selected = b_dense[columns]
        products = jnp.einsum("nxy,njyz->njxz", values, selected, precision=highest)
        onehot = ((local_rows[:, None] == jnp.arange(BR, dtype=jnp.int32)[None, :]) & alive_mask[:, None]).astype(jnp.float32)
        return jnp.einsum("ni,njxz->ijxz", onehot, products, precision=highest)

    slabs = lax.map(grid_row, (a_vals, a_row, a_col, live_slots))
    product_full = slabs.reshape(NBLK, NBLK, BLK, BLK)
    return product_full * c_keep.astype(jnp.float32)[:, :, None, None]
```

```python
import jax
import jax.numpy as jnp
from jax import lax
from jax.experimental import pallas as pl
from jax.experimental.pallas import tpu as pltpu
from jax.sharding import PartitionSpec as P

BLK = 92
LANES = 128
ROWS = 96
HALF = 48
PACKED = ROWS + HALF
REST = LANES - BLK
TAIL = BLK - REST
N_Z = 16
ZERO = 64
F32 = jnp.float32
BF16 = jnp.bfloat16


def lanes_of(shape):
    return lax.broadcasted_iota(jnp.int32, shape, 1)


def pack_kernel(a_row, a_col, a_count, b_rows, a_ref, b_ref, pa_ref, pb_ref, pad):
    lane = lanes_of((ROWS, LANES))
    sub = lax.broadcasted_iota(jnp.int32, (8, LANES), 0)
    lane8 = lanes_of((8, LANES))
    for s in range(2):
        pa_ref[s] = jnp.zeros((ROWS, LANES), F32)
        pa_ref[s, :BLK, :BLK] = a_ref[:, s, :]
        row = jnp.where(s < a_count[0, 0], a_row[0, s], 2)
        col = a_col[0, s]
        last = pa_ref[s, ROWS - 8 :, :]
        index = jnp.where(lane8 == 0, col.astype(F32), row.astype(F32))
        pa_ref[s, ROWS - 8 :, :] = jnp.where((sub == 4) & (lane8 < 2), index, last)
    pad[...] = jnp.zeros((2, ROWS, LANES), F32)
    pad[0, :BLK, :BLK] = b_ref[:, 0, :]
    pad[1, :BLK, :BLK] = b_ref[:, 1, :]
    first, second = pad[0], pad[1]
    pb_ref[:ROWS] = jnp.where(lane < BLK, first, pltpu.roll(second, BLK, 1))
    rest = pltpu.roll(second, BLK, 1)
    low, high = rest[:HALF], pltpu.roll(rest[HALF:], TAIL, 1)
    lane = lanes_of((HALF, LANES))
    fold = jnp.where(lane < TAIL, low, high)
    fold = jnp.where(lane == 2 * TAIL, b_rows[0, 0].astype(F32), fold)
    fold = jnp.where(lane > 2 * TAIL, b_rows[0, 1].astype(F32), fold)
    pb_ref[ROWS:] = fold


def split(x):
    hi = x.astype(BF16)
    return hi, (x - hi.astype(F32)).astype(BF16)


def product_kernel(counts, a_index, b_index, keep, a_ref, *refs):
    pieces = refs[: len(counts)]
    out_ref, b_hi, b_lo, slots, cols, used, place = refs[len(counts) :]
    lane = lanes_of((ROWS, LANES))

    def clear(n, _):
        b_hi[n, ROWS:] = jnp.zeros((LANES - ROWS, LANES), BF16)
        b_lo[n, ROWS:] = jnp.zeros((LANES - ROWS, LANES), BF16)
        return 0

    lax.fori_loop(0, ZERO, clear, 0)
    b_hi[ZERO] = jnp.zeros((LANES, LANES), BF16)
    b_lo[ZERO] = jnp.zeros((LANES, LANES), BF16)

    def forget(n, _):
        place[0, n] = ZERO
        place[1, n] = ZERO
        return 0

    lax.fori_loop(0, ZERO, forget, 0)
    base = 0
    for piece, count in zip(pieces, counts):

        def unpack(c, _, piece=piece, base=base):
            body = piece[c, :ROWS]
            fold = piece[c, ROWS:]
            first = jnp.where(lane < BLK, body, 0.0)
            rest = jnp.concatenate([pltpu.roll(fold, REST, 1), pltpu.roll(fold, REST + LANES - BLK + REST, 1)], axis=0)
            second = jnp.where(lane < REST, pltpu.roll(body, REST, 1), jnp.where(lane < BLK, rest, 0.0))
            n = 2 * (base + c)
            for j, block in enumerate((first, second)):
                hi, lo = split(block)
                b_hi[n + j, :ROWS] = hi
                b_lo[n + j, :ROWS] = lo
                place[j, b_index[base + c, j]] = n + j
            return 0

        lax.fori_loop(0, count, unpack, 0)
        base += count

    for i in range(3):
        used[i] = 0

    def listed(n, _):
        i = a_index[n, 1]
        c = used[i]
        slots[i, c] = n
        cols[i, c] = a_index[n, 0]
        used[i] = c + 1
        return 0

    lax.fori_loop(0, a_ref.shape[0], listed, 0)

    for i in range(2):

        def pair(q, total, i=i):
            both, high = total
            parts_hi, parts_lo, rows_hi, rows_lo = [], [], [], []
            for t in range(2):
                hi, lo = split(a_ref[slots[i, 2 * q + t]])
                parts_hi.append(hi)
                parts_lo.append(lo)
                k = cols[i, 2 * q + t]
                p0, p1 = place[0, k], place[1, k]
                rows_hi.append(jnp.concatenate([b_hi[p0], b_hi[p1]], axis=1))
                rows_lo.append(jnp.concatenate([b_lo[p0], b_lo[p1]], axis=1))
            a_hi = jnp.concatenate(parts_hi, axis=1)
            a_lo = jnp.concatenate(parts_lo, axis=1)
            k_hi = jnp.concatenate(rows_hi, axis=0)
            k_lo = jnp.concatenate(rows_lo, axis=0)
            both = both + jnp.dot(jnp.concatenate([a_hi, a_lo], axis=0), k_hi, preferred_element_type=F32)
            high = high + jnp.dot(a_hi, k_lo, preferred_element_type=F32)
            return both, high

        zero = (jnp.zeros((2 * ROWS, 2 * LANES), F32), jnp.zeros((ROWS, 2 * LANES), F32))
        both, high = lax.fori_loop(0, 8, pair, zero, unroll=True)
        total = both[:ROWS] + both[ROWS:] + high
        for j in range(2):
            kept = keep[i, j].astype(F32)
            out_ref[i, :, j, :] = total[:BLK, j * LANES : j * LANES + BLK] * kept


def shift_z(by):
    return [(2 * z + h, 2 * ((z + by) % N_Z) + h) for z in range(N_Z) for h in range(2)]


def spread(own):
    move = lambda x, perm: lax.ppermute(x, "row", perm)
    other = move(own, [(r, r ^ 1) for r in range(2 * N_Z)])
    pair = jnp.concatenate([own, other], axis=0)
    right, left, far = (move(pair, shift_z(by)) for by in (4, -4, 8))
    four = jnp.concatenate([pair, right, left, far], axis=0)
    return [
        four,
        move(four, shift_z(1)),
        move(four, shift_z(-1)),
        move(jnp.concatenate([pair, right], axis=0), shift_z(2)),
        move(jnp.concatenate([pair, left], axis=0), shift_z(-2)),
    ]


def per_device(a_vals, a_row, a_col, a_count, b_vals, b_rows, c_keep):
    smem = pl.BlockSpec(memory_space=pltpu.SMEM)
    vmem = pl.BlockSpec(memory_space=pltpu.VMEM)
    pa, pb = pl.pallas_call(
        pack_kernel,
        out_shape=(
            jax.ShapeDtypeStruct((2, ROWS, LANES), F32),
            jax.ShapeDtypeStruct((PACKED, LANES), F32),
        ),
        in_specs=[smem] * 4 + [vmem] * 2,
        out_specs=(vmem, vmem),
        scratch_shapes=[pltpu.VMEM((2, ROWS, LANES), F32)],
    )(a_row, a_col, a_count, b_rows, a_vals[0].transpose(1, 0, 2), b_vals[0].transpose(1, 0, 2))
    a_whole = lax.all_gather(pa, "col", axis=0, tiled=True)
    pieces = spread(pb[None])
    counts = [piece.shape[0] for piece in pieces]
    b_index = jnp.concatenate([piece[:, ROWS, 2 * TAIL : 2 * TAIL + 2] for piece in pieces], axis=0).astype(jnp.int32)
    a_index = a_whole[:, BLK, :2].astype(jnp.int32)
    return product(counts, a_index, b_index, c_keep, a_whole, pieces)


def product(counts, a_index, b_index, c_keep, a_whole, pieces):
    smem = pl.BlockSpec(memory_space=pltpu.SMEM)
    vmem = pl.BlockSpec(memory_space=pltpu.VMEM)
    out = pl.pallas_call(
        lambda *refs: product_kernel(counts, *refs),
        out_shape=jax.ShapeDtypeStruct((2, BLK, 2, BLK), F32),
        in_specs=[smem] * 3 + [vmem] * (1 + len(pieces)),
        out_specs=vmem,
        scratch_shapes=[
            pltpu.VMEM((ZERO + 1, LANES, LANES), BF16),
            pltpu.VMEM((ZERO + 1, LANES, LANES), BF16),
            pltpu.SMEM((3, 64), jnp.int32),
            pltpu.SMEM((3, 64), jnp.int32),
            pltpu.SMEM((3,), jnp.int32),
            pltpu.SMEM((2, ZERO), jnp.int32),
        ],
        compiler_params=pltpu.CompilerParams(vmem_limit_bytes=40 * 2**20),
    )(a_index, b_index, c_keep, a_whole, *pieces)
    return out.transpose(0, 2, 1, 3)


def solution(mesh):
    return jax.shard_map(
        per_device,
        mesh=mesh,
        in_specs=(
            P("row", "col", None, None),
            P("row", "col"),
            P("row", "col"),
            P("row", "col"),
            P("row", "col", None, None),
            P("row", "col"),
            P("row", "col"),
        ),
        out_specs=P("row", "col", None, None),
        check_vma=False,
    )
```

```python
import jax
import jax.numpy as jnp
from jax import lax
from jax.experimental import pallas as pl
from jax.experimental.pallas import tpu as pltpu
from jax.sharding import PartitionSpec as P

BLK = 92
LANES = 128
ROWS = 96
HALF = 48
PACKED = ROWS + HALF
REST = LANES - BLK
TAIL = BLK - REST
NOTE = 2 * TAIL
N_Z, N_Y = 16, 8
KA = 16
ZERO = 64
CHUNKS = 32
COPIES = 4
F32 = jnp.float32
BF16 = jnp.bfloat16
SMEM = pl.BlockSpec(memory_space=pltpu.SMEM)
VMEM = pl.BlockSpec(memory_space=pltpu.VMEM)


def lanes_of(shape):
    return lax.broadcasted_iota(jnp.int32, shape, 1)


def pack_into(out_ref, pad, src_ref, notes):
    for s in range(2):
        pad[s, :BLK, :BLK] = src_ref[:, s, :]
    first, second = pad[0], pad[1]
    shifted = pltpu.roll(second, BLK, 1)
    out_ref[:ROWS] = jnp.where(lanes_of((ROWS, LANES)) < BLK, first, shifted)
    low, high = shifted[:HALF], pltpu.roll(shifted[HALF:], TAIL, 1)
    lane = lanes_of((HALF, LANES))
    fold = jnp.where(lane < TAIL, low, high)
    for n, note in enumerate(notes):
        fold = jnp.where(lane == NOTE + n, note.astype(F32), fold)
    out_ref[ROWS:] = fold


def pack_kernel(a_row, a_col, a_count, b_rows, a_ref, b_ref, pa_ref, pb_ref, pad):
    pad[...] = jnp.zeros((2, ROWS, LANES), F32)
    notes = [a_col[0, 0], a_col[0, 1], a_row[0, 0], a_row[0, 1], a_count[0, 0]]
    pack_into(pa_ref, pad, a_ref, notes)
    pack_into(pb_ref, pad, b_ref, [b_rows[0, 0], b_rows[0, 1]])


def first_of(ref, c):
    return jnp.where(lanes_of((ROWS, LANES)) < BLK, ref[c, :ROWS], 0.0)


def second_of(ref, c):
    lane = lanes_of((ROWS, LANES))
    fold = ref[c, ROWS:]
    rest = jnp.concatenate([pltpu.roll(fold, REST, 1), pltpu.roll(fold, LANES - (TAIL - REST), 1)], axis=0)
    return jnp.where(lane < REST, pltpu.roll(ref[c, :ROWS], REST, 1), jnp.where(lane < BLK, rest, 0.0))


def split(x):
    hi = x.astype(BF16)
    return hi, (x - hi.astype(F32)).astype(BF16)


def product_kernel(counts, b_index, keep, a_any, *refs):
    pieces = refs[: len(counts)]
    out_ref, a_ref, a_both, b_hi, b_lo, a_note, cols, used, place, sems = refs[len(counts) :]
    step = CHUNKS // COPIES
    note_copy = pltpu.make_async_copy(a_any.at[:, pl.ds(ROWS, 8), :], a_note, sems.at[COPIES])
    note_copy.start()
    copies = [
        pltpu.make_async_copy(a_any.at[pl.ds(n * step, step)], a_ref.at[pl.ds(n * step, step)], sems.at[n])
        for n in range(COPIES)
    ]
    for copy in copies:
        copy.start()

    def clear(n, _):
        b_hi[n, ROWS:] = jnp.zeros((LANES - ROWS, LANES), BF16)
        b_lo[n, ROWS:] = jnp.zeros((LANES - ROWS, LANES), BF16)
        return 0

    lax.fori_loop(0, ZERO, clear, 0, unroll=4)
    b_hi[ZERO] = jnp.zeros((LANES, LANES), BF16)
    b_lo[ZERO] = jnp.zeros((LANES, LANES), BF16)

    def forget(n, _):
        place[0, n] = ZERO
        place[1, n] = ZERO
        return 0

    lax.fori_loop(0, ZERO, forget, 0)
    base = 0
    for piece, count in zip(pieces, counts):

        def unpack(c, _, piece=piece, base=base):
            n = 2 * (base + c)
            for j, block in enumerate((first_of(piece, c), second_of(piece, c))):
                hi, lo = split(block)
                b_hi[n + j, :ROWS] = hi
                b_lo[n + j, :ROWS] = lo
                place[j, b_index[base + c, j]] = n + j
            return 0

        lax.fori_loop(0, count, unpack, 0, unroll=2)
        base += count

    for i in range(2):
        used[i] = 0
    note_copy.wait()
    for copy in copies:
        copy.wait()

    def listed(c, _):
        count = a_note[c, 0, NOTE + 4].astype(jnp.int32)
        for s, taken in enumerate((first_of, second_of)):

            @pl.when(s < count)
            def _(s=s, taken=taken):
                i = a_note[c, 0, NOTE + 2 + s].astype(jnp.int32)
                q = used[i]
                cols[i, q] = a_note[c, 0, NOTE + s].astype(jnp.int32)
                used[i] = q + 1
                hi, lo = split(taken(a_ref, c))
                a_both[i, q, :ROWS] = hi
                a_both[i, q, ROWS:] = lo

        return 0

    lax.fori_loop(0, CHUNKS, listed, 0)

    for i in range(2):

        def pair(p, total, i=i):
            both, high = total
            rows_hi, rows_lo = [], []
            for t in range(2):
                k = cols[i, 2 * p + t]
                p0, p1 = place[0, k], place[1, k]
                rows_hi.append(jnp.concatenate([b_hi[p0], b_hi[p1]], axis=1))
                rows_lo.append(jnp.concatenate([b_lo[p0], b_lo[p1]], axis=1))
            a = jnp.concatenate([a_both[i, 2 * p], a_both[i, 2 * p + 1]], axis=1)
            both = both + jnp.dot(a, jnp.concatenate(rows_hi, axis=0), preferred_element_type=F32)
            high = high + jnp.dot(a[:ROWS], jnp.concatenate(rows_lo, axis=0), preferred_element_type=F32)
            return both, high

        zero = (jnp.zeros((2 * ROWS, 2 * LANES), F32), jnp.zeros((ROWS, 2 * LANES), F32))
        both, high = lax.fori_loop(0, KA // 2, pair, zero, unroll=True)
        total = both[:ROWS] + both[ROWS:] + high
        for j in range(2):
            kept = keep[i, j].astype(F32)
            out_ref[i, :, j, :] = total[:BLK, j * LANES : j * LANES + BLK] * kept


def gather(x, axis, groups):
    return lax.all_gather(x, axis, axis=0, tiled=True, axis_index_groups=groups)


def shift_z(by):
    return [(2 * z + h, 2 * ((z + by) % N_Z) + h) for z in range(N_Z) for h in range(2)]


def spread_a(own):
    plane = gather(own, "col", [[4 * y + k for k in range(4)] for y in range(N_Y)])
    return gather(plane, "col", [[4 * y + k for y in range(N_Y)] for k in range(4)])


def spread_b(own):
    cubes = [[2 * (4 * c + i) + h for c in range(N_Z // 4)] for i in range(4) for h in range(2)]
    four = gather(own, "row", cubes)
    eight = gather(four, "row", [[2 * z, 2 * z + 1] for z in range(N_Z)])
    move = lambda x, by: lax.ppermute(x, "row", shift_z(by))
    return [eight, move(eight, 1), move(eight, -1), move(eight[:4], -2), move(eight[4:], 2)]


def pack(a_vals, a_row, a_col, a_count, b_vals, b_rows):
    shape = jax.ShapeDtypeStruct((PACKED, LANES), F32)
    return pl.pallas_call(
        pack_kernel,
        out_shape=(shape, shape),
        in_specs=[SMEM] * 4 + [VMEM] * 2,
        out_specs=(VMEM, VMEM),
        scratch_shapes=[pltpu.VMEM((2, ROWS, LANES), F32)],
    )(a_row, a_col, a_count, b_rows, a_vals[0].transpose(1, 0, 2), b_vals[0].transpose(1, 0, 2))


def product(c_keep, a_whole, pieces):
    counts = [piece.shape[0] for piece in pieces]
    b_index = jnp.concatenate([piece[:, ROWS, NOTE : NOTE + 2] for piece in pieces], axis=0).astype(jnp.int32)
    out = pl.pallas_call(
        lambda *refs: product_kernel(counts, *refs),
        out_shape=jax.ShapeDtypeStruct((2, BLK, 2, BLK), F32),
        in_specs=[SMEM] * 2 + [pl.BlockSpec(memory_space=pltpu.HBM)] + [VMEM] * len(pieces),
        out_specs=VMEM,
        scratch_shapes=[
            pltpu.VMEM((CHUNKS, PACKED, LANES), F32),
            pltpu.VMEM((2, KA, 2 * ROWS, LANES), BF16),
            pltpu.VMEM((ZERO + 1, LANES, LANES), BF16),
            pltpu.VMEM((ZERO + 1, LANES, LANES), BF16),
            pltpu.SMEM((CHUNKS, 8, LANES), F32),
            pltpu.SMEM((2, KA), jnp.int32),
            pltpu.SMEM((2,), jnp.int32),
            pltpu.SMEM((2, ZERO), jnp.int32),
            pltpu.SemaphoreType.DMA((COPIES + 1,)),
        ],
        compiler_params=pltpu.CompilerParams(vmem_limit_bytes=40 * 2**20),
    )(b_index, c_keep, a_whole, *pieces)
    return out.transpose(0, 2, 1, 3)


def per_device(a_vals, a_row, a_col, a_count, b_vals, b_rows, c_keep):
    pa, pb = pack(a_vals, a_row, a_col, a_count, b_vals, b_rows)
    return product(c_keep, spread_a(pa[None]), spread_b(pb[None]))


def solution(mesh):
    return jax.shard_map(
        per_device,
        mesh=mesh,
        in_specs=(
            P("row", "col", None, None),
            P("row", "col"),
            P("row", "col"),
            P("row", "col"),
            P("row", "col", None, None),
            P("row", "col"),
            P("row", "col"),
        ),
        out_specs=P("row", "col", None, None),
        check_vma=False,
    )
```

```python
import jax
import jax.numpy as jnp
from jax import lax
from jax.experimental import pallas as pl
from jax.experimental.pallas import tpu as pltpu
from jax.sharding import PartitionSpec as P

BLK = 92
LANES = 128
ROWS = 96
HALF = 48
PACKED = ROWS + HALF
REST = LANES - BLK
TAIL = BLK - REST
NOTE = 2 * TAIL
N_Z, N_Y = 16, 8
KA = 16
ZERO = 64
CHUNKS = 32
COPIES = 4
F32 = jnp.float32
BF16 = jnp.bfloat16
SMEM = pl.BlockSpec(memory_space=pltpu.SMEM)
VMEM = pl.BlockSpec(memory_space=pltpu.VMEM)


def lanes_of(shape):
    return lax.broadcasted_iota(jnp.int32, shape, 1)


def pack_into(out_ref, pad, src_ref, notes):
    for s in range(2):
        pad[s, :BLK, :BLK] = src_ref[:, s, :]
    first, second = pad[0], pad[1]
    shifted = pltpu.roll(second, BLK, 1)
    out_ref[:ROWS] = jnp.where(lanes_of((ROWS, LANES)) < BLK, first, shifted)
    low, high = shifted[:HALF], pltpu.roll(shifted[HALF:], TAIL, 1)
    lane = lanes_of((HALF, LANES))
    fold = jnp.where(lane < TAIL, low, high)
    for n, note in enumerate(notes):
        fold = jnp.where(lane == NOTE + n, note.astype(F32), fold)
    out_ref[ROWS:] = fold


def pack_kernel(a_row, a_col, a_count, b_rows, a_ref, b_ref, pa_ref, pb_ref, pad):
    pad[...] = jnp.zeros((2, ROWS, LANES), F32)
    notes = [a_col[0, 0], a_col[0, 1], a_row[0, 0], a_row[0, 1], a_count[0, 0]]
    pack_into(pa_ref, pad, a_ref, notes)
    pack_into(pb_ref, pad, b_ref, [b_rows[0, 0], b_rows[0, 1]])


def first_of(ref, c):
    return jnp.where(lanes_of((ROWS, LANES)) < BLK, ref[c, :ROWS], 0.0)


def second_of(ref, c):
    lane = lanes_of((ROWS, LANES))
    fold = ref[c, ROWS:]
    rest = jnp.concatenate([pltpu.roll(fold, REST, 1), pltpu.roll(fold, LANES - (TAIL - REST), 1)], axis=0)
    return jnp.where(lane < REST, pltpu.roll(ref[c, :ROWS], REST, 1), jnp.where(lane < BLK, rest, 0.0))


def split(x):
    hi = x.astype(BF16)
    return hi, (x - hi.astype(F32)).astype(BF16)


def product_kernel(counts, b_index, keep, a_any, *refs):
    pieces = refs[: len(counts)]
    out_ref, a_ref, a_both, b_hi, b_lo, a_note, cols, used, place, sems = refs[len(counts) :]
    step = CHUNKS // COPIES
    note_copy = pltpu.make_async_copy(a_any.at[:, pl.ds(ROWS, 1), :], a_note, sems.at[COPIES])
    note_copy.start()
    copies = [
        pltpu.make_async_copy(a_any.at[pl.ds(n * step, step)], a_ref.at[pl.ds(n * step, step)], sems.at[n])
        for n in range(COPIES)
    ]
    for copy in copies:
        copy.start()

    def clear(n, _):
        b_hi[n, ROWS:] = jnp.zeros((LANES - ROWS, LANES), BF16)
        b_lo[n, ROWS:] = jnp.zeros((LANES - ROWS, LANES), BF16)
        return 0

    lax.fori_loop(0, ZERO, clear, 0, unroll=4)
    b_hi[ZERO] = jnp.zeros((LANES, LANES), BF16)
    b_lo[ZERO] = jnp.zeros((LANES, LANES), BF16)

    def forget(n, _):
        place[0, n] = ZERO
        place[1, n] = ZERO
        return 0

    lax.fori_loop(0, ZERO, forget, 0)
    base = 0
    for piece, count in zip(pieces, counts):

        def unpack(c, _, piece=piece, base=base):
            n = 2 * (base + c)
            for j, block in enumerate((first_of(piece, c), second_of(piece, c))):
                hi, lo = split(block)
                b_hi[n + j, :ROWS] = hi
                b_lo[n + j, :ROWS] = lo
                place[j, b_index[base + c, j]] = n + j
            return 0

        lax.fori_loop(0, count, unpack, 0, unroll=2)
        base += count

    for i in range(2):
        used[i] = 0
    note_copy.wait()
    for copy in copies:
        copy.wait()

    def listed(c, _):
        count = a_note[c, 0, NOTE + 4].astype(jnp.int32)
        for s, taken in enumerate((first_of, second_of)):

            @pl.when(s < count)
            def _(s=s, taken=taken):
                i = a_note[c, 0, NOTE + 2 + s].astype(jnp.int32)
                q = used[i]
                cols[i, q] = a_note[c, 0, NOTE + s].astype(jnp.int32)
                used[i] = q + 1
                hi, lo = split(taken(a_ref, c))
                a_both[i, q, :ROWS] = hi
                a_both[i, q, ROWS:] = lo

        return 0

    lax.fori_loop(0, CHUNKS, listed, 0)

    for i in range(2):

        def pair(p, total, i=i):
            both, high = total
            rows_hi, rows_lo = [], []
            for t in range(2):
                k = cols[i, 2 * p + t]
                p0, p1 = place[0, k], place[1, k]
                rows_hi.append(jnp.concatenate([b_hi[p0], b_hi[p1]], axis=1))
                rows_lo.append(jnp.concatenate([b_lo[p0], b_lo[p1]], axis=1))
            a = jnp.concatenate([a_both[i, 2 * p], a_both[i, 2 * p + 1]], axis=1)
            both = both + jnp.dot(a, jnp.concatenate(rows_hi, axis=0), preferred_element_type=F32)
            high = high + jnp.dot(a[:ROWS], jnp.concatenate(rows_lo, axis=0), preferred_element_type=F32)
            return both, high

        zero = (jnp.zeros((2 * ROWS, 2 * LANES), F32), jnp.zeros((ROWS, 2 * LANES), F32))
        both, high = lax.fori_loop(0, KA // 2, pair, zero, unroll=True)
        total = both[:ROWS] + both[ROWS:] + high
        for j in range(2):
            kept = keep[i, j].astype(F32)
            out_ref[i, :, j, :] = total[:BLK, j * LANES : j * LANES + BLK] * kept


def gather(x, axis, groups):
    return lax.all_gather(x, axis, axis=0, tiled=True, axis_index_groups=groups)


def shift_z(by):
    return [(2 * z + h, 2 * ((z + by) % N_Z) + h) for z in range(N_Z) for h in range(2)]


def spread_a(own):
    plane = gather(own, "col", [[4 * y + k for k in range(4)] for y in range(N_Y)])
    return gather(plane, "col", [[4 * y + k for y in range(N_Y)] for k in range(4)])


def spread_b(own):
    cubes = [[2 * (4 * c + i) + h for c in range(N_Z // 4)] for i in range(4) for h in range(2)]
    move = lambda x, perm: lax.ppermute(x, "row", perm)
    across = [(r, r ^ 1) for r in range(2 * N_Z)]
    four = gather(own, "row", cubes)
    far = [move(four[:2], shift_z(-2)), move(four[2:], shift_z(2))]
    other = move(four, across)
    near = [move(x, shift_z(by)) for x in (four, other) for by in (1, -1)]
    return [four, other, *near, *far, move(jnp.concatenate(far, axis=0), across)]


def pack(a_vals, a_row, a_col, a_count, b_vals, b_rows):
    shape = jax.ShapeDtypeStruct((PACKED, LANES), F32)
    return pl.pallas_call(
        pack_kernel,
        out_shape=(shape, shape),
        in_specs=[SMEM] * 4 + [VMEM] * 2,
        out_specs=(VMEM, VMEM),
        scratch_shapes=[pltpu.VMEM((2, ROWS, LANES), F32)],
    )(a_row, a_col, a_count, b_rows, a_vals[0].transpose(1, 0, 2), b_vals[0].transpose(1, 0, 2))


def product(c_keep, a_whole, pieces):
    counts = [piece.shape[0] for piece in pieces]
    b_index = jnp.concatenate([piece[:, ROWS, NOTE : NOTE + 2] for piece in pieces], axis=0).astype(jnp.int32)
    out = pl.pallas_call(
        lambda *refs: product_kernel(counts, *refs),
        out_shape=jax.ShapeDtypeStruct((2, BLK, 2, BLK), F32),
        in_specs=[SMEM] * 2 + [pl.BlockSpec(memory_space=pltpu.HBM)] + [VMEM] * len(pieces),
        out_specs=VMEM,
        scratch_shapes=[
            pltpu.VMEM((CHUNKS, PACKED, LANES), F32),
            pltpu.VMEM((2, KA, 2 * ROWS, LANES), BF16),
            pltpu.VMEM((ZERO + 1, LANES, LANES), BF16),
            pltpu.VMEM((ZERO + 1, LANES, LANES), BF16),
            pltpu.SMEM((CHUNKS, 1, LANES), F32),
            pltpu.SMEM((2, KA), jnp.int32),
            pltpu.SMEM((2,), jnp.int32),
            pltpu.SMEM((2, ZERO), jnp.int32),
            pltpu.SemaphoreType.DMA((COPIES + 1,)),
        ],
        compiler_params=pltpu.CompilerParams(vmem_limit_bytes=40 * 2**20),
    )(b_index, c_keep, a_whole, *pieces)
    return out.transpose(0, 2, 1, 3)


def per_device(a_vals, a_row, a_col, a_count, b_vals, b_rows, c_keep):
    pa, pb = pack(a_vals, a_row, a_col, a_count, b_vals, b_rows)
    return product(c_keep, spread_a(pa[None]), spread_b(pb[None]))


def solution(mesh):
    return jax.shard_map(
        per_device,
        mesh=mesh,
        in_specs=(
            P("row", "col", None, None),
            P("row", "col"),
            P("row", "col"),
            P("row", "col"),
            P("row", "col", None, None),
            P("row", "col"),
            P("row", "col"),
        ),
        out_specs=P("row", "col", None, None),
        check_vma=False,
    )
```

```python
import jax
import jax.numpy as jnp
from jax import lax
from jax.experimental import pallas as pl
from jax.experimental.pallas import tpu as pltpu
from jax.sharding import PartitionSpec as P

BLK = 92
LANES = 128
ROWS = 96
HALF = 48
PACKED = ROWS + HALF
REST = LANES - BLK
TAIL = BLK - REST
NOTE = 2 * TAIL
N_Z, N_Y = 16, 8
KA = 16
ZERO = 64
CHUNKS = 32
F32 = jnp.float32
BF16 = jnp.bfloat16
SMEM = pl.BlockSpec(memory_space=pltpu.SMEM)
VMEM = pl.BlockSpec(memory_space=pltpu.VMEM)
SMALL = pltpu.CompilerParams(vmem_limit_bytes=2 * 2**20)


def lanes_of(shape):
    return lax.broadcasted_iota(jnp.int32, shape, 1)


def pack_into(out_ref, pad, src_ref, notes):
    for s in range(2):
        pad[s, :BLK, :BLK] = src_ref[:, s, :]
    first, second = pad[0], pad[1]
    shifted = pltpu.roll(second, BLK, 1)
    out_ref[:ROWS] = jnp.where(lanes_of((ROWS, LANES)) < BLK, first, shifted)
    low, high = shifted[:HALF], pltpu.roll(shifted[HALF:], TAIL, 1)
    lane = lanes_of((HALF, LANES))
    fold = jnp.where(lane < TAIL, low, high)
    for n, note in enumerate(notes):
        fold = jnp.where(lane == NOTE + n, note.astype(F32), fold)
    out_ref[ROWS:] = fold


def pack_kernel(a_row, a_col, a_count, b_rows, a_ref, b_ref, pa_ref, pb_ref, pad):
    pad[...] = jnp.zeros((2, ROWS, LANES), F32)
    notes = [a_col[0, 0], a_col[0, 1], a_row[0, 0], a_row[0, 1], a_count[0, 0]]
    pack_into(pa_ref, pad, a_ref, notes)
    pack_into(pb_ref, pad, b_ref, [b_rows[0, 0], b_rows[0, 1]])


def first_of(ref, c):
    return jnp.where(lanes_of((ROWS, LANES)) < BLK, ref[c, :ROWS], 0.0)


def second_of(ref, c):
    lane = lanes_of((ROWS, LANES))
    fold = ref[c, ROWS:]
    rest = jnp.concatenate([pltpu.roll(fold, REST, 1), pltpu.roll(fold, LANES - (TAIL - REST), 1)], axis=0)
    return jnp.where(lane < REST, pltpu.roll(ref[c, :ROWS], REST, 1), jnp.where(lane < BLK, rest, 0.0))


def split(x):
    hi = x.astype(BF16)
    return hi, (x - hi.astype(F32)).astype(BF16)


def product_kernel(n_a, counts, keep, *refs):
    pieces = refs[: len(counts)]
    out_ref, a_both, b_hi, b_lo, notes, cols, used, place, sems = refs[len(counts) :]
    starts = [sum(counts[:n]) for n in range(len(counts))]
    copies = [
        pltpu.make_async_copy(piece.at[:, pl.ds(ROWS, 1), :], notes.at[pl.ds(start, count)], sems.at[n])
        for n, (piece, start, count) in enumerate(zip(pieces, starts, counts))
    ]
    for copy in copies:
        copy.start()

    def clear(n, _):
        b_hi[n, ROWS:] = jnp.zeros((LANES - ROWS, LANES), BF16)
        b_lo[n, ROWS:] = jnp.zeros((LANES - ROWS, LANES), BF16)
        return 0

    lax.fori_loop(0, ZERO, clear, 0, unroll=4)
    b_hi[ZERO] = jnp.zeros((LANES, LANES), BF16)
    b_lo[ZERO] = jnp.zeros((LANES, LANES), BF16)

    def forget(n, _):
        place[0, n] = ZERO
        place[1, n] = ZERO
        return 0

    lax.fori_loop(0, ZERO, forget, 0)
    for i in range(2):
        used[i] = 0
    for copy in copies:
        copy.wait()

    for piece, start, count in zip(pieces[n_a:], starts[n_a:], counts[n_a:]):

        def unpack(c, _, piece=piece, start=start):
            n = 2 * (start + c - CHUNKS)
            for j, block in enumerate((first_of(piece, c), second_of(piece, c))):
                hi, lo = split(block)
                b_hi[n + j, :ROWS] = hi
                b_lo[n + j, :ROWS] = lo
                place[j, notes[start + c, 0, NOTE + j].astype(jnp.int32)] = n + j
            return 0

        lax.fori_loop(0, count, unpack, 0, unroll=2)

    for piece, start, count in zip(pieces[:n_a], starts[:n_a], counts[:n_a]):

        def listed(c, _, piece=piece, start=start):
            live = notes[start + c, 0, NOTE + 4].astype(jnp.int32)
            for s, taken in enumerate((first_of, second_of)):

                @pl.when(s < live)
                def _(s=s, taken=taken):
                    i = notes[start + c, 0, NOTE + 2 + s].astype(jnp.int32)
                    q = used[i]
                    cols[i, q] = notes[start + c, 0, NOTE + s].astype(jnp.int32)
                    used[i] = q + 1
                    hi, lo = split(taken(piece, c))
                    a_both[i, q, :ROWS] = hi
                    a_both[i, q, ROWS:] = lo

            return 0

        lax.fori_loop(0, count, listed, 0)

    for i in range(2):

        def pair(p, total, i=i):
            both, high = total
            rows_hi, rows_lo = [], []
            for t in range(2):
                k = cols[i, 2 * p + t]
                p0, p1 = place[0, k], place[1, k]
                rows_hi.append(jnp.concatenate([b_hi[p0], b_hi[p1]], axis=1))
                rows_lo.append(jnp.concatenate([b_lo[p0], b_lo[p1]], axis=1))
            a = jnp.concatenate([a_both[i, 2 * p], a_both[i, 2 * p + 1]], axis=1)
            both = both + jnp.dot(a, jnp.concatenate(rows_hi, axis=0), preferred_element_type=F32)
            high = high + jnp.dot(a[:ROWS], jnp.concatenate(rows_lo, axis=0), preferred_element_type=F32)
            return both, high

        zero = (jnp.zeros((2 * ROWS, 2 * LANES), F32), jnp.zeros((ROWS, 2 * LANES), F32))
        both, high = lax.fori_loop(0, KA // 2, pair, zero, unroll=True)
        total = both[:ROWS] + both[ROWS:] + high
        for j in range(2):
            kept = keep[i, j].astype(F32)
            out_ref[i, :, j, :] = total[:BLK, j * LANES : j * LANES + BLK] * kept


def join_kernel(n_parts, *refs):
    at = 0
    for ref in refs[:n_parts]:
        count = ref.shape[0]
        refs[-1][at : at + count] = ref[...]
        at += count


def join(*parts, after=()):
    return pl.pallas_call(
        lambda *refs: join_kernel(len(parts), *refs),
        out_shape=jax.ShapeDtypeStruct((sum(part.shape[0] for part in parts), PACKED, LANES), F32),
        in_specs=[VMEM] * len(parts) + [pl.BlockSpec(memory_space=pl.ANY)] * len(after),
        out_specs=VMEM,
        compiler_params=SMALL,
    )(*parts, *after)


def pairs(bit):
    return [(n, n ^ bit) for n in range(32)]


def shifts(count, stride, by):
    return [(stride * n + k, stride * ((n + by) % count) + k) for n in range(count) for k in range(stride)]


def spread(a_own, b_own):
    in_row = lambda x, perm: lax.ppermute(x, "row", perm)
    in_col = lambda x, perm: lax.ppermute(x, "col", perm)

    beside = in_col(a_own, pairs(2))
    far = [in_row(b_own, shifts(N_Z, 2, by)) for by in (8, 4, -4)]
    two = join(a_own, beside, after=far[:1])
    a_four = join(two, in_col(two, shifts(N_Y, 4, N_Y // 2)), after=far[1:])
    b_four = join(b_own, *far)

    b_second = in_row(b_four, pairs(4))
    b_first = in_row(b_four, pairs(2))
    b_third = in_row(b_second, pairs(2))
    b_other = [in_row(b_four, pairs(1))]
    b_other += [in_row(some, pairs(1)) for some in (join(b_second, b_first, after=b_other), b_third)]

    a_second = in_col(a_four, pairs(8))
    a_first = in_col(a_four, pairs(4))
    a_third = in_col(a_second, pairs(4))
    a_other = [in_col(join(*some), pairs(1)) for some in ((a_four, a_second), (a_first, a_third))]
    return [a_four, a_second, a_first, a_third, *a_other], [b_four, b_second, b_first, b_third, *b_other]


def pack(a_vals, a_row, a_col, a_count, b_vals, b_rows):
    shape = jax.ShapeDtypeStruct((PACKED, LANES), F32)
    return pl.pallas_call(
        pack_kernel,
        out_shape=(shape, shape),
        in_specs=[SMEM] * 4 + [VMEM] * 2,
        out_specs=(VMEM, VMEM),
        scratch_shapes=[pltpu.VMEM((2, ROWS, LANES), F32)],
    )(a_row, a_col, a_count, b_rows, a_vals[0].transpose(1, 0, 2), b_vals[0].transpose(1, 0, 2))


def product(c_keep, a_pieces, b_pieces):
    pieces = [*a_pieces, *b_pieces]
    counts = [piece.shape[0] for piece in pieces]
    out = pl.pallas_call(
        lambda *refs: product_kernel(len(a_pieces), counts, *refs),
        out_shape=jax.ShapeDtypeStruct((2, BLK, 2, BLK), F32),
        in_specs=[SMEM] + [VMEM] * len(pieces),
        out_specs=VMEM,
        scratch_shapes=[
            pltpu.VMEM((2, KA, 2 * ROWS, LANES), BF16),
            pltpu.VMEM((ZERO + 1, LANES, LANES), BF16),
            pltpu.VMEM((ZERO + 1, LANES, LANES), BF16),
            pltpu.SMEM((2 * CHUNKS, 1, LANES), F32),
            pltpu.SMEM((2, KA), jnp.int32),
            pltpu.SMEM((2,), jnp.int32),
            pltpu.SMEM((2, ZERO), jnp.int32),
            pltpu.SemaphoreType.DMA((len(pieces),)),
        ],
        compiler_params=pltpu.CompilerParams(vmem_limit_bytes=32 * 2**20),
    )(c_keep, *pieces)
    return out.transpose(0, 2, 1, 3)


def per_device(a_vals, a_row, a_col, a_count, b_vals, b_rows, c_keep):
    pa, pb = pack(a_vals, a_row, a_col, a_count, b_vals, b_rows)
    return product(c_keep, *spread(pa[None], pb[None]))


def solution(mesh):
    return jax.shard_map(
        per_device,
        mesh=mesh,
        in_specs=(
            P("row", "col", None, None),
            P("row", "col"),
            P("row", "col"),
            P("row", "col"),
            P("row", "col", None, None),
            P("row", "col"),
            P("row", "col"),
        ),
        out_specs=P("row", "col", None, None),
        check_vma=False,
    )
```

```python
import jax
import jax.numpy as jnp
from jax import lax
from jax.experimental import pallas as pl
from jax.experimental.pallas import tpu as pltpu
from jax.sharding import PartitionSpec as P

BLK = 92
LANES = 128
ROWS = 96
HALF = 48
PACKED = ROWS + HALF
REST = LANES - BLK
TAIL = BLK - REST
NOTE = 2 * TAIL
N_Z, N_Y = 16, 8
KA = 16
ZERO = 64
CHUNKS = 32
F32 = jnp.float32
BF16 = jnp.bfloat16
SMEM = pl.BlockSpec(memory_space=pltpu.SMEM)
VMEM = pl.BlockSpec(memory_space=pltpu.VMEM)
SMALL = pltpu.CompilerParams(vmem_limit_bytes=2 * 2**20)


def lanes_of(shape):
    return lax.broadcasted_iota(jnp.int32, shape, 1)


def pack_into(out_ref, pad, src_ref, notes):
    for s in range(2):
        pad[s, :BLK, :BLK] = src_ref[:, s, :]
    first, second = pad[0], pad[1]
    shifted = pltpu.roll(second, BLK, 1)
    out_ref[:ROWS] = jnp.where(lanes_of((ROWS, LANES)) < BLK, first, shifted)
    low, high = shifted[:HALF], pltpu.roll(shifted[HALF:], TAIL, 1)
    lane = lanes_of((HALF, LANES))
    fold = jnp.where(lane < TAIL, low, high)
    for n, note in enumerate(notes):
        fold = jnp.where(lane == NOTE + n, note.astype(F32), fold)
    out_ref[ROWS:] = fold


def pack_kernel(a_row, a_col, a_count, b_rows, a_ref, b_ref, pa_ref, pb_ref, pad):
    pad[...] = jnp.zeros((2, ROWS, LANES), F32)
    notes = [a_col[0, 0], a_col[0, 1], a_row[0, 0], a_row[0, 1], a_count[0, 0]]
    pack_into(pa_ref, pad, a_ref, notes)
    pack_into(pb_ref, pad, b_ref, [b_rows[0, 0], b_rows[0, 1]])


def first_of(ref, c):
    return jnp.where(lanes_of((ROWS, LANES)) < BLK, ref[c, :ROWS], 0.0)


def second_of(ref, c):
    lane = lanes_of((ROWS, LANES))
    fold = ref[c, ROWS:]
    rest = jnp.concatenate([pltpu.roll(fold, REST, 1), pltpu.roll(fold, LANES - (TAIL - REST), 1)], axis=0)
    return jnp.where(lane < REST, pltpu.roll(ref[c, :ROWS], REST, 1), jnp.where(lane < BLK, rest, 0.0))


def split(x):
    hi = x.astype(BF16)
    return hi, (x - hi.astype(F32)).astype(BF16)


def product_kernel(n_a, counts, keep, *refs):
    pieces = refs[: len(counts)]
    out_ref, a_both, b_hi, b_lo, notes, cols, used, place, sems = refs[len(counts) :]
    starts = [sum(counts[:n]) for n in range(len(counts))]
    copies = [
        pltpu.make_async_copy(piece.at[:, pl.ds(ROWS, 1), :], notes.at[pl.ds(start, count)], sems.at[n])
        for n, (piece, start, count) in enumerate(zip(pieces, starts, counts))
    ]
    for copy in copies:
        copy.start()

    def clear(n, _):
        b_hi[n, ROWS:] = jnp.zeros((LANES - ROWS, LANES), BF16)
        b_lo[n, ROWS:] = jnp.zeros((LANES - ROWS, LANES), BF16)
        return 0

    lax.fori_loop(0, ZERO, clear, 0, unroll=4)
    b_hi[ZERO] = jnp.zeros((LANES, LANES), BF16)
    b_lo[ZERO] = jnp.zeros((LANES, LANES), BF16)

    def forget(n, _):
        place[0, n] = ZERO
        place[1, n] = ZERO
        return 0

    lax.fori_loop(0, ZERO, forget, 0)
    for i in range(2):
        used[i] = 0
    for copy in copies:
        copy.wait()

    for piece, start, count in zip(pieces[n_a:], starts[n_a:], counts[n_a:]):

        def unpack(c, _, piece=piece, start=start):
            n = 2 * (start + c - CHUNKS)
            for j, block in enumerate((first_of(piece, c), second_of(piece, c))):
                hi, lo = split(block)
                b_hi[n + j, :ROWS] = hi
                b_lo[n + j, :ROWS] = lo
                place[j, notes[start + c, 0, NOTE + j].astype(jnp.int32)] = n + j
            return 0

        lax.fori_loop(0, count, unpack, 0, unroll=2)

    for piece, start, count in zip(pieces[:n_a], starts[:n_a], counts[:n_a]):

        def listed(c, _, piece=piece, start=start):
            live = notes[start + c, 0, NOTE + 4].astype(jnp.int32)
            for s, taken in enumerate((first_of, second_of)):

                @pl.when(s < live)
                def _(s=s, taken=taken):
                    i = notes[start + c, 0, NOTE + 2 + s].astype(jnp.int32)
                    q = used[i]
                    cols[i, q] = notes[start + c, 0, NOTE + s].astype(jnp.int32)
                    used[i] = q + 1
                    hi, lo = split(taken(piece, c))
                    a_both[i, q, :ROWS] = hi
                    a_both[i, q, ROWS:] = lo

            return 0

        lax.fori_loop(0, count, listed, 0)

    for i in range(2):

        def pair(p, total, i=i):
            both, high = total
            rows_hi, rows_lo = [], []
            for t in range(2):
                k = cols[i, 2 * p + t]
                p0, p1 = place[0, k], place[1, k]
                rows_hi.append(jnp.concatenate([b_hi[p0], b_hi[p1]], axis=1))
                rows_lo.append(jnp.concatenate([b_lo[p0], b_lo[p1]], axis=1))
            a = jnp.concatenate([a_both[i, 2 * p], a_both[i, 2 * p + 1]], axis=1)
            both = both + jnp.dot(a, jnp.concatenate(rows_hi, axis=0), preferred_element_type=F32)
            high = high + jnp.dot(a[:ROWS], jnp.concatenate(rows_lo, axis=0), preferred_element_type=F32)
            return both, high

        zero = (jnp.zeros((2 * ROWS, 2 * LANES), F32), jnp.zeros((ROWS, 2 * LANES), F32))
        both, high = lax.fori_loop(0, KA // 2, pair, zero, unroll=True)
        total = both[:ROWS] + both[ROWS:] + high
        for j in range(2):
            kept = keep[i, j].astype(F32)
            out_ref[i, :, j, :] = total[:BLK, j * LANES : j * LANES + BLK] * kept


def join_kernel(n_parts, *refs):
    at = 0
    for ref in refs[:n_parts]:
        count = ref.shape[0]
        refs[-1][at : at + count] = ref[...]
        at += count


def join(*parts, after=()):
    return pl.pallas_call(
        lambda *refs: join_kernel(len(parts), *refs),
        out_shape=jax.ShapeDtypeStruct((sum(part.shape[0] for part in parts), PACKED, LANES), F32),
        in_specs=[VMEM] * len(parts) + [pl.BlockSpec(memory_space=pl.ANY)] * len(after),
        out_specs=VMEM,
        compiler_params=SMALL,
    )(*parts, *after)


def pairs(bit):
    return [(n, n ^ bit) for n in range(32)]


def shifts(count, stride, by):
    return [(stride * n + k, stride * ((n + by) % count) + k) for n in range(count) for k in range(stride)]


def spread(a_own, b_own):
    in_row = lambda x, perm: lax.ppermute(x, "row", perm)
    in_col = lambda x, perm: lax.ppermute(x, "col", perm)

    beside = in_col(a_own, pairs(2))
    cubes = [[2 * (4 * c + i) + h for c in range(N_Z // 4)] for i in range(4) for h in range(2)]
    b_four = lax.all_gather(b_own, "row", axis=0, tiled=True, axis_index_groups=cubes)
    two = join(a_own, beside)
    a_far = in_col(two, shifts(N_Y, 4, N_Y // 2))

    b_second = in_row(b_four, pairs(4))
    b_first = in_row(b_four, pairs(2))
    b_third = in_row(b_second, pairs(2))
    b_other = [in_row(some, pairs(1)) for some in (b_four, b_first, b_second, b_third)]

    a_four = join(two, a_far, after=[b_four])
    a_second = in_col(a_four, pairs(8))
    a_first = in_col(a_four, pairs(4))
    a_third = in_col(join(a_second, after=[b_first, b_other[0]]), pairs(4))
    a_halves = [join(a_four, a_second, after=b_other[1:2]), join(a_first, a_third, after=[b_third, b_other[2]])]
    a_other = [in_col(half, pairs(1)) for half in a_halves]
    return [a_four, a_second, a_first, a_third, *a_other], [b_four, b_second, b_first, b_third, *b_other]


def pack(a_vals, a_row, a_col, a_count, b_vals, b_rows):
    shape = jax.ShapeDtypeStruct((PACKED, LANES), F32)
    return pl.pallas_call(
        pack_kernel,
        out_shape=(shape, shape),
        in_specs=[SMEM] * 4 + [VMEM] * 2,
        out_specs=(VMEM, VMEM),
        scratch_shapes=[pltpu.VMEM((2, ROWS, LANES), F32)],
    )(a_row, a_col, a_count, b_rows, a_vals[0].transpose(1, 0, 2), b_vals[0].transpose(1, 0, 2))


def product(c_keep, a_pieces, b_pieces):
    pieces = [*a_pieces, *b_pieces]
    counts = [piece.shape[0] for piece in pieces]
    out = pl.pallas_call(
        lambda *refs: product_kernel(len(a_pieces), counts, *refs),
        out_shape=jax.ShapeDtypeStruct((2, BLK, 2, BLK), F32),
        in_specs=[SMEM] + [VMEM] * len(pieces),
        out_specs=VMEM,
        scratch_shapes=[
            pltpu.VMEM((2, KA, 2 * ROWS, LANES), BF16),
            pltpu.VMEM((ZERO + 1, LANES, LANES), BF16),
            pltpu.VMEM((ZERO + 1, LANES, LANES), BF16),
            pltpu.SMEM((2 * CHUNKS, 1, LANES), F32),
            pltpu.SMEM((2, KA), jnp.int32),
            pltpu.SMEM((2,), jnp.int32),
            pltpu.SMEM((2, ZERO), jnp.int32),
            pltpu.SemaphoreType.DMA((len(pieces),)),
        ],
        compiler_params=pltpu.CompilerParams(vmem_limit_bytes=32 * 2**20),
    )(c_keep, *pieces)
    return out.transpose(0, 2, 1, 3)


def per_device(a_vals, a_row, a_col, a_count, b_vals, b_rows, c_keep):
    pa, pb = pack(a_vals, a_row, a_col, a_count, b_vals, b_rows)
    return product(c_keep, *spread(pa[None], pb[None]))


def solution(mesh):
    return jax.shard_map(
        per_device,
        mesh=mesh,
        in_specs=(
            P("row", "col", None, None),
            P("row", "col"),
            P("row", "col"),
            P("row", "col"),
            P("row", "col", None, None),
            P("row", "col"),
            P("row", "col"),
        ),
        out_specs=P("row", "col", None, None),
        check_vma=False,
    )
```

```python
import jax
import jax.numpy as jnp
from jax import lax
from jax.experimental import pallas as pl
from jax.experimental.pallas import tpu as pltpu
from jax.sharding import PartitionSpec as P

BLK = 92
LANES = 128
ROWS = 96
HALF = 48
PACKED = ROWS + HALF
REST = LANES - BLK
TAIL = BLK - REST
NOTE = 2 * TAIL
N_Z, N_Y = 16, 8
KA = 16
ZERO = 64
CHUNKS = 32
F32 = jnp.float32
BF16 = jnp.bfloat16
SMEM = pl.BlockSpec(memory_space=pltpu.SMEM)
VMEM = pl.BlockSpec(memory_space=pltpu.VMEM)
SMALL = pltpu.CompilerParams(vmem_limit_bytes=2 * 2**20)


def lanes_of(shape):
    return lax.broadcasted_iota(jnp.int32, shape, 1)


def pack_into(out_ref, pad, src_ref, notes):
    for s in range(2):
        pad[s, :BLK, :BLK] = src_ref[:, s, :]
    first, second = pad[0], pad[1]
    shifted = pltpu.roll(second, BLK, 1)
    out_ref[:ROWS] = jnp.where(lanes_of((ROWS, LANES)) < BLK, first, shifted)
    low, high = shifted[:HALF], pltpu.roll(shifted[HALF:], TAIL, 1)
    lane = lanes_of((HALF, LANES))
    fold = jnp.where(lane < TAIL, low, high)
    for n, note in enumerate(notes):
        fold = jnp.where(lane == NOTE + n, note.astype(F32), fold)
    out_ref[ROWS:] = fold


def pack_kernel(a_row, a_col, a_count, b_rows, a_ref, b_ref, pa_ref, pb_ref, pad):
    pad[...] = jnp.zeros((2, ROWS, LANES), F32)
    notes = [a_col[0, 0], a_col[0, 1], a_row[0, 0], a_row[0, 1], a_count[0, 0]]
    pack_into(pa_ref, pad, a_ref, notes)
    pack_into(pb_ref, pad, b_ref, [b_rows[0, 0], b_rows[0, 1]])


def first_of(ref, c):
    return jnp.where(lanes_of((ROWS, LANES)) < BLK, ref[c, :ROWS], 0.0)


def second_of(ref, c):
    lane = lanes_of((ROWS, LANES))
    fold = ref[c, ROWS:]
    rest = jnp.concatenate([pltpu.roll(fold, REST, 1), pltpu.roll(fold, LANES - (TAIL - REST), 1)], axis=0)
    return jnp.where(lane < REST, pltpu.roll(ref[c, :ROWS], REST, 1), jnp.where(lane < BLK, rest, 0.0))


def split(x):
    hi = x.astype(BF16)
    return hi, (x - hi.astype(F32)).astype(BF16)


def product_kernel(n_a, counts, keep, *refs):
    pieces = refs[: len(counts)]
    out_ref, a_both, b_hi, b_lo, notes, cols, used, place, sems = refs[len(counts) :]
    starts = [sum(counts[:n]) for n in range(len(counts))]
    copies = [
        pltpu.make_async_copy(piece.at[:, pl.ds(ROWS, 1), :], notes.at[pl.ds(start, count)], sems.at[n])
        for n, (piece, start, count) in enumerate(zip(pieces, starts, counts))
    ]
    for copy in copies:
        copy.start()

    def clear(n, _):
        b_hi[n, ROWS:] = jnp.zeros((LANES - ROWS, LANES), BF16)
        b_lo[n, ROWS:] = jnp.zeros((LANES - ROWS, LANES), BF16)
        return 0

    lax.fori_loop(0, ZERO, clear, 0, unroll=4)
    b_hi[ZERO] = jnp.zeros((LANES, LANES), BF16)
    b_lo[ZERO] = jnp.zeros((LANES, LANES), BF16)

    def forget(n, _):
        place[0, n] = ZERO
        place[1, n] = ZERO
        return 0

    lax.fori_loop(0, ZERO, forget, 0)
    for i in range(2):
        used[i] = 0
    for copy in copies:
        copy.wait()

    for piece, start, count in zip(pieces[n_a:], starts[n_a:], counts[n_a:]):

        def unpack(c, _, piece=piece, start=start):
            n = 2 * (start + c - CHUNKS)
            for j, block in enumerate((first_of(piece, c), second_of(piece, c))):
                hi, lo = split(block)
                b_hi[n + j, :ROWS] = hi
                b_lo[n + j, :ROWS] = lo
                place[j, notes[start + c, 0, NOTE + j].astype(jnp.int32)] = n + j
            return 0

        lax.fori_loop(0, count, unpack, 0, unroll=2)

    for piece, start, count in zip(pieces[:n_a], starts[:n_a], counts[:n_a]):

        def listed(c, _, piece=piece, start=start):
            live = notes[start + c, 0, NOTE + 4].astype(jnp.int32)
            for s, taken in enumerate((first_of, second_of)):

                @pl.when(s < live)
                def _(s=s, taken=taken):
                    i = notes[start + c, 0, NOTE + 2 + s].astype(jnp.int32)
                    q = used[i]
                    cols[i, q] = notes[start + c, 0, NOTE + s].astype(jnp.int32)
                    used[i] = q + 1
                    hi, lo = split(taken(piece, c))
                    a_both[i, q, :ROWS] = hi
                    a_both[i, q, ROWS:] = lo

            return 0

        lax.fori_loop(0, count, listed, 0)

    for i in range(2):

        def pair(p, total, i=i):
            both, high = total
            rows_hi, rows_lo = [], []
            for t in range(2):
                k = cols[i, 2 * p + t]
                p0, p1 = place[0, k], place[1, k]
                rows_hi.append(jnp.concatenate([b_hi[p0], b_hi[p1]], axis=1))
                rows_lo.append(jnp.concatenate([b_lo[p0], b_lo[p1]], axis=1))
            a = jnp.concatenate([a_both[i, 2 * p], a_both[i, 2 * p + 1]], axis=1)
            both = both + jnp.dot(a, jnp.concatenate(rows_hi, axis=0), preferred_element_type=F32)
            high = high + jnp.dot(a[:ROWS], jnp.concatenate(rows_lo, axis=0), preferred_element_type=F32)
            return both, high

        zero = (jnp.zeros((2 * ROWS, 2 * LANES), F32), jnp.zeros((ROWS, 2 * LANES), F32))
        both, high = lax.fori_loop(0, KA // 2, pair, zero, unroll=True)
        total = both[:ROWS] + both[ROWS:] + high
        for j in range(2):
            kept = keep[i, j].astype(F32)
            out_ref[i, :, j, :] = total[:BLK, j * LANES : j * LANES + BLK] * kept


def join_kernel(n_parts, *refs):
    at = 0
    for ref in refs[:n_parts]:
        count = ref.shape[0]
        refs[-1][at : at + count] = ref[...]
        at += count


def join(*parts, after=()):
    return pl.pallas_call(
        lambda *refs: join_kernel(len(parts), *refs),
        out_shape=jax.ShapeDtypeStruct((sum(part.shape[0] for part in parts), PACKED, LANES), F32),
        in_specs=[VMEM] * len(parts) + [pl.BlockSpec(memory_space=pl.ANY)] * len(after),
        out_specs=VMEM,
        compiler_params=SMALL,
    )(*parts, *after)


def pairs(bit):
    return [(n, n ^ bit) for n in range(32)]


def shifts(count, stride, by):
    return [(stride * n + k, stride * ((n + by) % count) + k) for n in range(count) for k in range(stride)]


def spread(a_own, b_own):
    in_row = lambda x, perm: lax.ppermute(x, "row", perm)
    in_col = lambda x, perm: lax.ppermute(x, "col", perm)

    two = lax.all_gather(a_own, "col", axis=0, tiled=True, axis_index_groups=[[n, n + 2] for n in range(32) if not n & 2])
    a_far = in_col(two, shifts(N_Y, 4, N_Y // 2))
    cubes = [[2 * (4 * c + i) + h for c in range(N_Z // 4)] for i in range(4) for h in range(2)]
    b_four = lax.all_gather(b_own, "row", axis=0, tiled=True, axis_index_groups=cubes)

    b_other = in_row(b_four, pairs(1))
    b_second = in_row(b_four, pairs(4))
    b_first = in_row(b_four, pairs(2))
    b_third = in_row(b_second, pairs(2))
    others = [b_other, in_row(b_second, pairs(1)), in_row(b_other, pairs(2)), in_row(b_other, pairs(6))]

    a_four = join(two, a_far, after=[b_four])
    a_second = in_col(a_four, pairs(8))
    a_first = in_col(a_four, pairs(4))
    a_third = in_col(join(a_second, after=[b_first, b_other]), pairs(4))
    a_halves = [join(a_four, a_second), join(a_first, a_third, after=[b_third, *others[1:]])]
    a_other = [in_col(half, pairs(1)) for half in a_halves]
    return [a_four, a_second, a_first, a_third, *a_other], [b_four, b_second, b_first, b_third, *others]


def pack(a_vals, a_row, a_col, a_count, b_vals, b_rows):
    shape = jax.ShapeDtypeStruct((PACKED, LANES), F32)
    return pl.pallas_call(
        pack_kernel,
        out_shape=(shape, shape),
        in_specs=[SMEM] * 4 + [VMEM] * 2,
        out_specs=(VMEM, VMEM),
        scratch_shapes=[pltpu.VMEM((2, ROWS, LANES), F32)],
    )(a_row, a_col, a_count, b_rows, a_vals[0].transpose(1, 0, 2), b_vals[0].transpose(1, 0, 2))


def product(c_keep, a_pieces, b_pieces):
    pieces = [*a_pieces, *b_pieces]
    counts = [piece.shape[0] for piece in pieces]
    out = pl.pallas_call(
        lambda *refs: product_kernel(len(a_pieces), counts, *refs),
        out_shape=jax.ShapeDtypeStruct((2, BLK, 2, BLK), F32),
        in_specs=[SMEM] + [VMEM] * len(pieces),
        out_specs=VMEM,
        scratch_shapes=[
            pltpu.VMEM((2, KA, 2 * ROWS, LANES), BF16),
            pltpu.VMEM((ZERO + 1, LANES, LANES), BF16),
            pltpu.VMEM((ZERO + 1, LANES, LANES), BF16),
            pltpu.SMEM((2 * CHUNKS, 1, LANES), F32),
            pltpu.SMEM((2, KA), jnp.int32),
            pltpu.SMEM((2,), jnp.int32),
            pltpu.SMEM((2, ZERO), jnp.int32),
            pltpu.SemaphoreType.DMA((len(pieces),)),
        ],
        compiler_params=pltpu.CompilerParams(vmem_limit_bytes=32 * 2**20),
    )(c_keep, *pieces)
    return out.transpose(0, 2, 1, 3)


def per_device(a_vals, a_row, a_col, a_count, b_vals, b_rows, c_keep):
    pa, pb = pack(a_vals, a_row, a_col, a_count, b_vals, b_rows)
    return product(c_keep, *spread(pa[None], pb[None]))


def solution(mesh):
    return jax.shard_map(
        per_device,
        mesh=mesh,
        in_specs=(
            P("row", "col", None, None),
            P("row", "col"),
            P("row", "col"),
            P("row", "col"),
            P("row", "col", None, None),
            P("row", "col"),
            P("row", "col"),
        ),
        out_specs=P("row", "col", None, None),
        check_vma=False,
    )
```

```python
import jax
import jax.numpy as jnp
from jax import lax
from jax.experimental import pallas as pl
from jax.experimental.pallas import tpu as pltpu
from jax.sharding import PartitionSpec as P

BLK = 92
LANES = 128
ROWS = 96
HALF = 48
PACKED = ROWS + HALF
REST = LANES - BLK
TAIL = BLK - REST
NOTE = 2 * TAIL
N_Z, N_Y = 16, 8
KA = 16
NBLK = 64
CHUNKS = 32
F32 = jnp.float32
BF16 = jnp.bfloat16
SMEM = pl.BlockSpec(memory_space=pltpu.SMEM)
VMEM = pl.BlockSpec(memory_space=pltpu.VMEM)
LARGE = pltpu.CompilerParams(vmem_limit_bytes=32 * 2**20)


def lanes_of(shape):
    return lax.broadcasted_iota(jnp.int32, shape, 1)


def pack_into(out_ref, pad, src_ref, notes):
    for s in range(2):
        pad[s, :BLK, :BLK] = src_ref[:, s, :]
    first, second = pad[0], pad[1]
    shifted = pltpu.roll(second, BLK, 1)
    out_ref[:ROWS] = jnp.where(lanes_of((ROWS, LANES)) < BLK, first, shifted)
    low, high = shifted[:HALF], pltpu.roll(shifted[HALF:], TAIL, 1)
    lane = lanes_of((HALF, LANES))
    fold = jnp.where(lane < TAIL, low, high)
    for n, note in enumerate(notes):
        fold = jnp.where(lane == NOTE + n, note.astype(F32), fold)
    out_ref[ROWS:] = fold


def pack_kernel(a_row, a_col, a_count, b_rows, a_ref, b_ref, pa_ref, pb_ref, pad):
    pad[...] = jnp.zeros((2, ROWS, LANES), F32)
    notes = [a_col[0, 0], a_col[0, 1], a_row[0, 0], a_row[0, 1], a_count[0, 0]]
    pack_into(pa_ref, pad, a_ref, notes)
    pack_into(pb_ref, pad, b_ref, [b_rows[0, 0], b_rows[0, 1]])


def first_of(ref, c):
    return jnp.where(lanes_of((ROWS, LANES)) < BLK, ref[c, :ROWS], 0.0)


def second_of(ref, c):
    lane = lanes_of((ROWS, LANES))
    fold = ref[c, ROWS:]
    rest = jnp.concatenate([pltpu.roll(fold, REST, 1), pltpu.roll(fold, LANES - (TAIL - REST), 1)], axis=0)
    return jnp.where(lane < REST, pltpu.roll(ref[c, :ROWS], REST, 1), jnp.where(lane < BLK, rest, 0.0))


def split(x):
    hi = x.astype(BF16)
    return hi, (x - hi.astype(F32)).astype(BF16)


def start_notes(pieces, counts, notes, sems):
    copies, start = [], 0
    for n, (piece, count) in enumerate(zip(pieces, counts)):
        copies.append(pltpu.make_async_copy(piece.at[:, pl.ds(ROWS, 1), :], notes.at[pl.ds(start, count)], sems.at[n]))
        copies[-1].start()
        start += count
    return copies


def prepare_a(piece, notes, start, a_both, cols, used):
    for i in range(2):
        used[i] = 0

    def listed(c, _):
        live = notes[start + c, 0, NOTE + 4].astype(jnp.int32)
        for s, taken in enumerate((first_of, second_of)):

            @pl.when(s < live)
            def _(s=s, taken=taken):
                i = notes[start + c, 0, NOTE + 2 + s].astype(jnp.int32)
                q = used[i]
                cols[i, q] = notes[start + c, 0, NOTE + s].astype(jnp.int32)
                used[i] = q + 1
                hi, lo = split(taken(piece, c))
                a_both[i, q, :ROWS] = hi
                a_both[i, q, ROWS:] = lo

        return 0

    lax.fori_loop(0, CHUNKS, listed, 0)


def prepare_b(pieces, counts, notes, b_hi, b_lo, place):
    zero = 2 * sum(counts)

    def clear(n, _):
        b_hi[n, ROWS:] = jnp.zeros((LANES - ROWS, LANES), BF16)
        b_lo[n, ROWS:] = jnp.zeros((LANES - ROWS, LANES), BF16)
        return 0

    lax.fori_loop(0, zero, clear, 0, unroll=4)
    b_hi[zero] = jnp.zeros((LANES, LANES), BF16)
    b_lo[zero] = jnp.zeros((LANES, LANES), BF16)

    def forget(n, _):
        place[0, n] = zero
        place[1, n] = zero
        return 0

    lax.fori_loop(0, NBLK, forget, 0, unroll=8)
    start = 0
    for piece, count in zip(pieces, counts):

        def unpack(c, _, piece=piece, start=start):
            n = 2 * (start + c)
            for j, block in enumerate((first_of(piece, c), second_of(piece, c))):
                hi, lo = split(block)
                b_hi[n + j, :ROWS] = hi
                b_lo[n + j, :ROWS] = lo
                place[j, notes[start + c, 0, NOTE + j].astype(jnp.int32)] = n + j
            return 0

        lax.fori_loop(0, count, unpack, 0, unroll=2)
        start += count


def products(i, a_both, cols, b_hi, b_lo, place):
    def pair(p, total):
        both, high = total
        rows_hi, rows_lo = [], []
        for t in range(2):
            k = cols[i, 2 * p + t]
            p0, p1 = place[0, k], place[1, k]
            rows_hi.append(jnp.concatenate([b_hi[p0], b_hi[p1]], axis=1))
            rows_lo.append(jnp.concatenate([b_lo[p0], b_lo[p1]], axis=1))
        a = jnp.concatenate([a_both[i, 2 * p], a_both[i, 2 * p + 1]], axis=1)
        both = both + jnp.dot(a, jnp.concatenate(rows_hi, axis=0), preferred_element_type=F32)
        high = high + jnp.dot(a[:ROWS], jnp.concatenate(rows_lo, axis=0), preferred_element_type=F32)
        return both, high

    zero = (jnp.zeros((2 * ROWS, 2 * LANES), F32), jnp.zeros((ROWS, 2 * LANES), F32))
    both, high = lax.fori_loop(0, KA // 2, pair, zero, unroll=True)
    return both[:ROWS] + both[ROWS:] + high


def early_kernel(counts, a_ref, *refs):
    pieces = refs[: len(counts)]
    a_both, cols, part_ref, b_hi, b_lo, notes, used, place, sems = refs[len(counts) :]
    copies = start_notes([*pieces, a_ref], [*counts, CHUNKS], notes, sems)
    for copy in copies:
        copy.wait()
    prepare_b(pieces, counts, notes, b_hi, b_lo, place)
    prepare_a(a_ref, notes, sum(counts), a_both, cols, used)
    for i in range(2):
        part_ref[i] = products(i, a_both, cols, b_hi, b_lo, place)


def late_kernel(counts, keep, cols, a_both, part_ref, *refs):
    pieces = refs[: len(counts)]
    out_ref, b_hi, b_lo, notes, place, sems = refs[len(counts) :]
    for copy in start_notes(pieces, counts, notes, sems):
        copy.wait()
    prepare_b(pieces, counts, notes, b_hi, b_lo, place)
    for i in range(2):
        total = part_ref[i] + products(i, a_both, cols, b_hi, b_lo, place)
        for j in range(2):
            kept = keep[i, j].astype(F32)
            out_ref[i, :, j, :] = total[:BLK, j * LANES : j * LANES + BLK] * kept


def pairs(bit):
    return [(n, n ^ bit) for n in range(32)]


def ring_pairs():
    return [(2 * z + h, 2 * ((z + (1 if z % 2 else -1)) % N_Z) + h) for z in range(N_Z) for h in range(2)]


def gather(x, axis, groups):
    return lax.all_gather(x, axis, axis=0, tiled=True, axis_index_groups=groups)


def spread_a(own):
    plane = gather(own, "col", [[4 * y + k for k in range(4)] for y in range(N_Y)])
    return gather(plane, "col", [[4 * y + k for y in range(N_Y)] for k in range(4)])


def spread_b(own):
    move = lambda x, perm: lax.ppermute(x, "row", perm)
    four = gather(own, "row", [[2 * (4 * c + i) + h for c in range(N_Z // 4)] for i in range(4) for h in range(2)])
    second = move(four, pairs(4))
    other = move(four, pairs(1))
    first = move(four, pairs(2))
    third = move(four, ring_pairs())
    late = [move(second, pairs(1)), move(other, pairs(2)), move(other, ring_pairs())]
    return [four, second, first, third, other], late


def pack(a_vals, a_row, a_col, a_count, b_vals, b_rows):
    shape = jax.ShapeDtypeStruct((PACKED, LANES), F32)
    return pl.pallas_call(
        pack_kernel,
        out_shape=(shape, shape),
        in_specs=[SMEM] * 4 + [VMEM] * 2,
        out_specs=(VMEM, VMEM),
        scratch_shapes=[pltpu.VMEM((2, ROWS, LANES), F32)],
    )(a_row, a_col, a_count, b_rows, a_vals[0].transpose(1, 0, 2), b_vals[0].transpose(1, 0, 2))


def scratch(counts):
    blocks = 2 * sum(counts) + 1
    return [pltpu.VMEM((blocks, LANES, LANES), BF16), pltpu.VMEM((blocks, LANES, LANES), BF16)]


def product(c_keep, a_whole, early, late):
    counts = [piece.shape[0] for piece in early]
    a_both, cols, part = pl.pallas_call(
        lambda *refs: early_kernel(counts, *refs),
        out_shape=(
            jax.ShapeDtypeStruct((2, KA, 2 * ROWS, LANES), BF16),
            jax.ShapeDtypeStruct((2, KA), jnp.int32),
            jax.ShapeDtypeStruct((2, ROWS, 2 * LANES), F32),
        ),
        in_specs=[VMEM] * (1 + len(early)),
        out_specs=(VMEM, SMEM, VMEM),
        scratch_shapes=[
            *scratch(counts),
            pltpu.SMEM((sum(counts) + CHUNKS, 1, LANES), F32),
            pltpu.SMEM((2,), jnp.int32),
            pltpu.SMEM((2, NBLK), jnp.int32),
            pltpu.SemaphoreType.DMA((len(early) + 1,)),
        ],
        compiler_params=LARGE,
    )(a_whole, *early)
    counts_late = [piece.shape[0] for piece in late]
    out = pl.pallas_call(
        lambda *refs: late_kernel(counts_late, *refs),
        out_shape=jax.ShapeDtypeStruct((2, BLK, 2, BLK), F32),
        in_specs=[SMEM] * 2 + [VMEM] * (2 + len(late)),
        out_specs=VMEM,
        scratch_shapes=[
            *scratch(counts_late),
            pltpu.SMEM((sum(counts_late), 1, LANES), F32),
            pltpu.SMEM((2, NBLK), jnp.int32),
            pltpu.SemaphoreType.DMA((len(late),)),
        ],
        compiler_params=LARGE,
    )(c_keep, cols, a_both, part, *late)
    return out.transpose(0, 2, 1, 3)


def per_device(a_vals, a_row, a_col, a_count, b_vals, b_rows, c_keep):
    pa, pb = pack(a_vals, a_row, a_col, a_count, b_vals, b_rows)
    return product(c_keep, spread_a(pa[None]), *spread_b(pb[None]))


def solution(mesh):
    return jax.shard_map(
        per_device,
        mesh=mesh,
        in_specs=(
            P("row", "col", None, None),
            P("row", "col"),
            P("row", "col"),
            P("row", "col"),
            P("row", "col", None, None),
            P("row", "col"),
            P("row", "col"),
        ),
        out_specs=P("row", "col", None, None),
        check_vma=False,
    )
```

```python
import jax
import jax.numpy as jnp
from jax import lax
from jax.experimental import pallas as pl
from jax.experimental.pallas import tpu as pltpu
from jax.sharding import PartitionSpec as P

BLK = 92
LANES = 128
ROWS = 96
HALF = 48
PACKED = ROWS + HALF
REST = LANES - BLK
TAIL = BLK - REST
NOTE = 2 * TAIL
N_Z, N_Y = 16, 8
KA = 16
NBLK = 64
CHUNKS = 32
F32 = jnp.float32
BF16 = jnp.bfloat16
SMEM = pl.BlockSpec(memory_space=pltpu.SMEM)
VMEM = pl.BlockSpec(memory_space=pltpu.VMEM)
LARGE = pltpu.CompilerParams(vmem_limit_bytes=32 * 2**20)
EARLY = pltpu.CompilerParams(vmem_limit_bytes=99 * 2**19)


def lanes_of(shape):
    return lax.broadcasted_iota(jnp.int32, shape, 1)


def pack_into(out_ref, pad, src_ref, notes):
    for s in range(2):
        pad[s, :BLK, :BLK] = src_ref[:, s, :]
    first, second = pad[0], pad[1]
    shifted = pltpu.roll(second, BLK, 1)
    out_ref[:ROWS] = jnp.where(lanes_of((ROWS, LANES)) < BLK, first, shifted)
    low, high = shifted[:HALF], pltpu.roll(shifted[HALF:], TAIL, 1)
    lane = lanes_of((HALF, LANES))
    fold = jnp.where(lane < TAIL, low, high)
    for n, note in enumerate(notes):
        fold = jnp.where(lane == NOTE + n, note.astype(F32), fold)
    out_ref[ROWS:] = fold


def pack_kernel(a_row, a_col, a_count, b_rows, a_ref, b_ref, pa_ref, pb_ref, pad):
    pad[...] = jnp.zeros((2, ROWS, LANES), F32)
    notes = [a_col[0, 0], a_col[0, 1], a_row[0, 0], a_row[0, 1], a_count[0, 0]]
    pack_into(pa_ref, pad, a_ref, notes)
    pack_into(pb_ref, pad, b_ref, [b_rows[0, 0], b_rows[0, 1]])


def first_of(ref, c):
    return jnp.where(lanes_of((ROWS, LANES)) < BLK, ref[c, :ROWS], 0.0)


def second_of(ref, c):
    lane = lanes_of((ROWS, LANES))
    fold = ref[c, ROWS:]
    rest = jnp.concatenate([pltpu.roll(fold, REST, 1), pltpu.roll(fold, LANES - (TAIL - REST), 1)], axis=0)
    return jnp.where(lane < REST, pltpu.roll(ref[c, :ROWS], REST, 1), jnp.where(lane < BLK, rest, 0.0))


def split(x):
    hi = x.astype(BF16)
    return hi, (x - hi.astype(F32)).astype(BF16)


def start_notes(pieces, counts, notes, sems):
    copies, start = [], 0
    for n, (piece, count) in enumerate(zip(pieces, counts)):
        copies.append(pltpu.make_async_copy(piece.at[:, pl.ds(ROWS, 1), :], notes.at[pl.ds(start, count)], sems.at[n]))
        copies[-1].start()
        start += count
    return copies


def padded(x):
    return jnp.concatenate([x, jnp.zeros((LANES - ROWS, LANES), BF16)], axis=0)


def prepare_a(piece, notes, start, a_both, cols, used):
    for i in range(2):
        used[i] = 0

    def listed(c, _):
        live = notes[start + c, 0, NOTE + 4].astype(jnp.int32)
        for s, taken in enumerate((first_of, second_of)):

            @pl.when(s < live)
            def _(s=s, taken=taken):
                i = notes[start + c, 0, NOTE + 2 + s].astype(jnp.int32)
                q = used[i]
                cols[i, q] = notes[start + c, 0, NOTE + s].astype(jnp.int32)
                used[i] = q + 1
                hi, lo = split(taken(piece, c))
                a_both[i, q, :ROWS] = hi
                a_both[i, q, ROWS:] = lo

        return 0

    lax.fori_loop(0, CHUNKS, listed, 0, unroll=8)


def forget(place, zero):
    def one(n, _):
        place[0, n] = zero
        place[1, n] = zero
        return 0

    lax.fori_loop(0, NBLK, one, 0, unroll=8)


def place_b(total, notes, place):
    forget(place, 2 * total)

    def one(c, _):
        for j in range(2):
            place[j, notes[c, 0, NOTE + j].astype(jnp.int32)] = 2 * c + j
        return 0

    lax.fori_loop(0, total, one, 0, unroll=4)


def prepare_b(pieces, counts, b_hi, b_lo):
    zero = 2 * sum(counts)
    b_hi[zero] = jnp.zeros((LANES, LANES), BF16)
    b_lo[zero] = jnp.zeros((LANES, LANES), BF16)
    start = 0
    for piece, count in zip(pieces, counts):

        def unpack(c, _, piece=piece, start=start):
            n = 2 * (start + c)
            for j, block in enumerate((first_of(piece, c), second_of(piece, c))):
                hi, lo = split(block)
                b_hi[n + j] = padded(hi)
                b_lo[n + j] = padded(lo)
            return 0

        lax.fori_loop(0, count, unpack, 0, unroll=4)
        start += count


def products(i, a_both, cols, b_hi, b_lo, place):
    def pair(p, total):
        both, high = total
        rows_hi, rows_lo = [], []
        for t in range(2):
            k = cols[i, 2 * p + t]
            p0, p1 = place[0, k], place[1, k]
            rows_hi.append(jnp.concatenate([b_hi[p0], b_hi[p1]], axis=1))
            rows_lo.append(jnp.concatenate([b_lo[p0], b_lo[p1]], axis=1))
        a = jnp.concatenate([a_both[i, 2 * p], a_both[i, 2 * p + 1]], axis=1)
        both = both + jnp.dot(a, jnp.concatenate(rows_hi, axis=0), preferred_element_type=F32)
        high = high + jnp.dot(a[:ROWS], jnp.concatenate(rows_lo, axis=0), preferred_element_type=F32)
        return both, high

    zero = (jnp.zeros((2 * ROWS, 2 * LANES), F32), jnp.zeros((ROWS, 2 * LANES), F32))
    both, high = lax.fori_loop(0, KA // 2, pair, zero, unroll=True)
    return both[:ROWS] + both[ROWS:] + high


def early_kernel(counts, a_any, *refs):
    pieces = refs[: len(counts)]
    a_both, cols, part_ref, a_ref, b_hi, b_lo, notes, used, place, sems = refs[len(counts) :]
    a_copy = pltpu.make_async_copy(a_any, a_ref, sems.at[len(counts) + 1])
    copies = start_notes([*pieces, a_any], [*counts, CHUNKS], notes, sems)
    a_copy.start()
    prepare_b(pieces, counts, b_hi, b_lo)
    for copy in copies:
        copy.wait()
    place_b(sum(counts), notes, place)
    a_copy.wait()
    prepare_a(a_ref, notes, sum(counts), a_both, cols, used)
    for i in range(2):
        part_ref[i] = products(i, a_both, cols, b_hi, b_lo, place)


def late_kernel(counts, keep, cols, a_both, part_ref, *refs):
    pieces = refs[: len(counts)]
    out_ref, b_hi, b_lo, notes, place, sems = refs[len(counts) :]
    copies = start_notes(pieces, counts, notes, sems)
    prepare_b(pieces, counts, b_hi, b_lo)
    for copy in copies:
        copy.wait()
    place_b(sum(counts), notes, place)
    for i in range(2):
        total = part_ref[i] + products(i, a_both, cols, b_hi, b_lo, place)
        for j in range(2):
            kept = keep[i, j].astype(F32)
            out_ref[i, :, j, :] = total[:BLK, j * LANES : j * LANES + BLK] * kept


def pairs(bit):
    return [(n, n ^ bit) for n in range(32)]


def ring_pairs():
    return [(2 * z + h, 2 * ((z + (1 if z % 2 else -1)) % N_Z) + h) for z in range(N_Z) for h in range(2)]


def gather(x, axis, groups):
    return lax.all_gather(x, axis, axis=0, tiled=True, axis_index_groups=groups)


def spread_a(own):
    plane = gather(own, "col", [[4 * y + k for k in range(4)] for y in range(N_Y)])
    return gather(plane, "col", [[4 * y + k for y in range(N_Y)] for k in range(4)])


def spread_b(own):
    move = lambda x, perm: lax.ppermute(x, "row", perm)
    four = gather(own, "row", [[2 * (4 * c + i) + h for c in range(N_Z // 4)] for i in range(4) for h in range(2)])
    second = move(four, pairs(4))
    other = move(four, pairs(1))
    first = move(four, pairs(2))
    third = move(four, ring_pairs())
    late = [move(second, pairs(1)), move(other, pairs(2)), move(other, ring_pairs())]
    return [four, second, first, third, other], late


def pack(a_vals, a_row, a_col, a_count, b_vals, b_rows):
    shape = jax.ShapeDtypeStruct((PACKED, LANES), F32)
    return pl.pallas_call(
        pack_kernel,
        out_shape=(shape, shape),
        in_specs=[SMEM] * 4 + [VMEM] * 2,
        out_specs=(VMEM, VMEM),
        scratch_shapes=[pltpu.VMEM((2, ROWS, LANES), F32)],
    )(a_row, a_col, a_count, b_rows, a_vals[0].transpose(1, 0, 2), b_vals[0].transpose(1, 0, 2))


def scratch(counts):
    blocks = 2 * sum(counts) + 1
    return [pltpu.VMEM((blocks, LANES, LANES), BF16), pltpu.VMEM((blocks, LANES, LANES), BF16)]


def product(c_keep, a_whole, early, late):
    counts = [piece.shape[0] for piece in early]
    a_both, cols, part = pl.pallas_call(
        lambda *refs: early_kernel(counts, *refs),
        out_shape=(
            jax.ShapeDtypeStruct((2, KA, 2 * ROWS, LANES), BF16),
            jax.ShapeDtypeStruct((2, KA), jnp.int32),
            jax.ShapeDtypeStruct((2, ROWS, 2 * LANES), F32),
        ),
        in_specs=[pl.BlockSpec(memory_space=pltpu.HBM)] + [VMEM] * len(early),
        out_specs=(VMEM, SMEM, VMEM),
        scratch_shapes=[
            pltpu.VMEM((CHUNKS, PACKED, LANES), F32),
            *scratch(counts),
            pltpu.SMEM((sum(counts) + CHUNKS, 1, LANES), F32),
            pltpu.SMEM((2,), jnp.int32),
            pltpu.SMEM((2, NBLK), jnp.int32),
            pltpu.SemaphoreType.DMA((len(early) + 2,)),
        ],
        compiler_params=EARLY,
    )(a_whole, *early)
    counts_late = [piece.shape[0] for piece in late]
    out = pl.pallas_call(
        lambda *refs: late_kernel(counts_late, *refs),
        out_shape=jax.ShapeDtypeStruct((2, BLK, 2, BLK), F32),
        in_specs=[SMEM] * 2 + [VMEM] * (2 + len(late)),
        out_specs=VMEM,
        scratch_shapes=[
            *scratch(counts_late),
            pltpu.SMEM((sum(counts_late), 1, LANES), F32),
            pltpu.SMEM((2, NBLK), jnp.int32),
            pltpu.SemaphoreType.DMA((len(late),)),
        ],
        compiler_params=LARGE,
    )(c_keep, cols, a_both, part, *late)
    return out.transpose(0, 2, 1, 3)


def per_device(a_vals, a_row, a_col, a_count, b_vals, b_rows, c_keep):
    pa, pb = pack(a_vals, a_row, a_col, a_count, b_vals, b_rows)
    return product(c_keep, spread_a(pa[None]), *spread_b(pb[None]))


def solution(mesh):
    return jax.shard_map(
        per_device,
        mesh=mesh,
        in_specs=(
            P("row", "col", None, None),
            P("row", "col"),
            P("row", "col"),
            P("row", "col"),
            P("row", "col", None, None),
            P("row", "col"),
            P("row", "col"),
        ),
        out_specs=P("row", "col", None, None),
        check_vma=False,
    )
```

```python
import jax
import jax.numpy as jnp
from jax import lax
from jax.experimental import pallas as pl
from jax.experimental.pallas import tpu as pltpu
from jax.sharding import PartitionSpec as P

BLK = 92
LANES = 128
ROWS = 96
HALF = 48
PACKED = ROWS + HALF
REST = LANES - BLK
TAIL = BLK - REST
NOTE = 2 * TAIL
N_Z, N_Y = 16, 8
KA = 16
NBLK = 64
CHUNKS = 32
F32 = jnp.float32
BF16 = jnp.bfloat16
SMEM = pl.BlockSpec(memory_space=pltpu.SMEM)
VMEM = pl.BlockSpec(memory_space=pltpu.VMEM)
LARGE = pltpu.CompilerParams(vmem_limit_bytes=32 * 2**20)
EARLY = pltpu.CompilerParams(vmem_limit_bytes=99 * 2**19)


def lanes_of(shape):
    return lax.broadcasted_iota(jnp.int32, shape, 1)


def pack_into(out_ref, pad, src_ref, notes):
    for s in range(2):
        pad[s, :BLK, :BLK] = src_ref[:, s, :]
    first, second = pad[0], pad[1]
    shifted = pltpu.roll(second, BLK, 1)
    out_ref[:ROWS] = jnp.where(lanes_of((ROWS, LANES)) < BLK, first, shifted)
    low, high = shifted[:HALF], pltpu.roll(shifted[HALF:], TAIL, 1)
    lane = lanes_of((HALF, LANES))
    fold = jnp.where(lane < TAIL, low, high)
    for n, note in enumerate(notes):
        fold = jnp.where(lane == NOTE + n, note.astype(F32), fold)
    out_ref[ROWS:] = fold


def pack_kernel(a_row, a_col, a_count, b_rows, a_ref, b_ref, pa_ref, pb_ref, pad):
    pad[...] = jnp.zeros((2, ROWS, LANES), F32)
    notes = [a_col[0, 0], a_col[0, 1], a_row[0, 0], a_row[0, 1], a_count[0, 0]]
    pack_into(pa_ref, pad, a_ref, notes)
    pack_into(pb_ref, pad, b_ref, [b_rows[0, 0], b_rows[0, 1]])


def first_of(ref, c):
    return jnp.where(lanes_of((ROWS, LANES)) < BLK, ref[c, :ROWS], 0.0)


def second_of(ref, c):
    lane = lanes_of((ROWS, LANES))
    fold = ref[c, ROWS:]
    rest = jnp.concatenate([pltpu.roll(fold, REST, 1), pltpu.roll(fold, LANES - (TAIL - REST), 1)], axis=0)
    return jnp.where(lane < REST, pltpu.roll(ref[c, :ROWS], REST, 1), jnp.where(lane < BLK, rest, 0.0))


def split(x):
    hi = x.astype(BF16)
    return hi, (x - hi.astype(F32)).astype(BF16)


def start_notes(pieces, counts, notes, sems):
    copies, start = [], 0
    for n, (piece, count) in enumerate(zip(pieces, counts)):
        copies.append(pltpu.make_async_copy(piece.at[:, pl.ds(ROWS, 1), :], notes.at[pl.ds(start, count)], sems.at[n]))
        copies[-1].start()
        start += count
    return copies


def padded(x):
    return jnp.concatenate([x, jnp.zeros((LANES - ROWS, LANES), BF16)], axis=0)


def prepare_a(piece, notes, start, a_both, cols, used):
    for i in range(2):
        used[i] = 0

    def listed(c, _):
        live = notes[start + c, 0, NOTE + 4].astype(jnp.int32)
        for s, taken in enumerate((first_of, second_of)):

            @pl.when(s < live)
            def _(s=s, taken=taken):
                i = notes[start + c, 0, NOTE + 2 + s].astype(jnp.int32)
                q = used[i]
                cols[i, q] = notes[start + c, 0, NOTE + s].astype(jnp.int32)
                used[i] = q + 1
                hi, lo = split(taken(piece, c))
                a_both[i, q, :ROWS] = hi
                a_both[i, q, ROWS:] = lo

        return 0

    lax.fori_loop(0, CHUNKS, listed, 0, unroll=8)


def forget(place, zero):
    def one(n, _):
        place[0, n] = zero
        place[1, n] = zero
        return 0

    lax.fori_loop(0, NBLK, one, 0, unroll=8)


def place_b(total, notes, place):
    forget(place, 2 * total)

    def one(c, _):
        for j in range(2):
            place[j, notes[c, 0, NOTE + j].astype(jnp.int32)] = 2 * c + j
        return 0

    lax.fori_loop(0, total, one, 0, unroll=4)


def prepare_b(pieces, counts, b_hi, b_lo):
    zero = 2 * sum(counts)
    b_hi[zero] = jnp.zeros((LANES, LANES), BF16)
    b_lo[zero] = jnp.zeros((LANES, LANES), BF16)
    start = 0
    for piece, count in zip(pieces, counts):

        def unpack(c, _, piece=piece, start=start):
            n = 2 * (start + c)
            for j, block in enumerate((first_of(piece, c), second_of(piece, c))):
                hi, lo = split(block)
                b_hi[n + j] = padded(hi)
                b_lo[n + j] = padded(lo)
            return 0

        lax.fori_loop(0, count, unpack, 0, unroll=4)
        start += count


def products(i, a_both, cols, b_hi, b_lo, place):
    def pair(p, total):
        both, high = total
        rows_hi, rows_lo = [], []
        for t in range(2):
            k = cols[i, 2 * p + t]
            p0, p1 = place[0, k], place[1, k]
            rows_hi.append(jnp.concatenate([b_hi[p0], b_hi[p1]], axis=1))
            rows_lo.append(jnp.concatenate([b_lo[p0], b_lo[p1]], axis=1))
        a = jnp.concatenate([a_both[i, 2 * p], a_both[i, 2 * p + 1]], axis=1)
        both = both + jnp.dot(a, jnp.concatenate(rows_hi, axis=0), preferred_element_type=F32)
        high = high + jnp.dot(a[:ROWS], jnp.concatenate(rows_lo, axis=0), preferred_element_type=F32)
        return both, high

    zero = (jnp.zeros((2 * ROWS, 2 * LANES), F32), jnp.zeros((ROWS, 2 * LANES), F32))
    both, high = lax.fori_loop(0, KA // 2, pair, zero, unroll=True)
    return both[:ROWS] + both[ROWS:] + high


def early_kernel(counts, a_any, *refs):
    pieces = refs[: len(counts)]
    a_both, cols, part_ref, a_ref, b_hi, b_lo, notes, used, place, sems = refs[len(counts) :]
    a_copy = pltpu.make_async_copy(a_any, a_ref, sems.at[len(counts) + 1])
    copies = start_notes([*pieces, a_any], [*counts, CHUNKS], notes, sems)
    a_copy.start()
    prepare_b(pieces, counts, b_hi, b_lo)
    for copy in copies:
        copy.wait()
    place_b(sum(counts), notes, place)
    a_copy.wait()
    prepare_a(a_ref, notes, sum(counts), a_both, cols, used)
    for i in range(2):
        part_ref[i] = products(i, a_both, cols, b_hi, b_lo, place)


def late_kernel(counts, keep, cols, a_both, part_ref, *refs):
    pieces = refs[: len(counts)]
    out_ref, b_hi, b_lo, notes, place, sems = refs[len(counts) :]
    copies = start_notes(pieces, counts, notes, sems)
    prepare_b(pieces, counts, b_hi, b_lo)
    for copy in copies:
        copy.wait()
    place_b(sum(counts), notes, place)
    for i in range(2):
        total = part_ref[i] + products(i, a_both, cols, b_hi, b_lo, place)
        for j in range(2):
            kept = keep[i, j].astype(F32)
            out_ref[i, :, j, :] = total[:BLK, j * LANES : j * LANES + BLK] * kept


def pairs(bit):
    return [(n, n ^ bit) for n in range(32)]


def ring_pairs():
    return [(2 * z + h, 2 * ((z + (1 if z % 2 else -1)) % N_Z) + h) for z in range(N_Z) for h in range(2)]


def gather(x, axis, groups):
    return lax.all_gather(x, axis, axis=0, tiled=True, axis_index_groups=groups)


def spread_a(own):
    plane = gather(own, "col", [[4 * y + k for k in range(4)] for y in range(N_Y)])
    return gather(plane, "col", [[4 * y + k for y in range(N_Y)] for k in range(4)])


def spread_b(own):
    move = lambda x, perm: lax.ppermute(x, "row", perm)
    half, step = N_Z // 2, N_Z // 4
    alike = [[2 * (4 * m + 2 * k + odd) + h for k in range(2) for m in range(step)] for odd in range(2) for h in range(2)]
    eight = gather(own, "row", alike)
    mine = step * (lax.axis_index("row") // 4 % 2)
    other = move(lax.dynamic_slice_in_dim(eight, mine, step), pairs(1))
    far = move(lax.dynamic_slice_in_dim(eight, half // 2 - mine, step), pairs(1))
    near = move(eight, pairs(2))
    return [eight, near, other, far], [move(other, pairs(2)), move(other, ring_pairs())]


def pack(a_vals, a_row, a_col, a_count, b_vals, b_rows):
    shape = jax.ShapeDtypeStruct((PACKED, LANES), F32)
    return pl.pallas_call(
        pack_kernel,
        out_shape=(shape, shape),
        in_specs=[SMEM] * 4 + [VMEM] * 2,
        out_specs=(VMEM, VMEM),
        scratch_shapes=[pltpu.VMEM((2, ROWS, LANES), F32)],
    )(a_row, a_col, a_count, b_rows, a_vals[0].transpose(1, 0, 2), b_vals[0].transpose(1, 0, 2))


def scratch(counts):
    blocks = 2 * sum(counts) + 1
    return [pltpu.VMEM((blocks, LANES, LANES), BF16), pltpu.VMEM((blocks, LANES, LANES), BF16)]


def product(c_keep, a_whole, early, late):
    counts = [piece.shape[0] for piece in early]
    a_both, cols, part = pl.pallas_call(
        lambda *refs: early_kernel(counts, *refs),
        out_shape=(
            jax.ShapeDtypeStruct((2, KA, 2 * ROWS, LANES), BF16),
            jax.ShapeDtypeStruct((2, KA), jnp.int32),
            jax.ShapeDtypeStruct((2, ROWS, 2 * LANES), F32),
        ),
        in_specs=[pl.BlockSpec(memory_space=pltpu.HBM)] + [VMEM] * len(early),
        out_specs=(VMEM, SMEM, VMEM),
        scratch_shapes=[
            pltpu.VMEM((CHUNKS, PACKED, LANES), F32),
            *scratch(counts),
            pltpu.SMEM((sum(counts) + CHUNKS, 1, LANES), F32),
            pltpu.SMEM((2,), jnp.int32),
            pltpu.SMEM((2, NBLK), jnp.int32),
            pltpu.SemaphoreType.DMA((len(early) + 2,)),
        ],
        compiler_params=EARLY,
    )(a_whole, *early)
    counts_late = [piece.shape[0] for piece in late]
    out = pl.pallas_call(
        lambda *refs: late_kernel(counts_late, *refs),
        out_shape=jax.ShapeDtypeStruct((2, BLK, 2, BLK), F32),
        in_specs=[SMEM] * 2 + [VMEM] * (2 + len(late)),
        out_specs=VMEM,
        scratch_shapes=[
            *scratch(counts_late),
            pltpu.SMEM((sum(counts_late), 1, LANES), F32),
            pltpu.SMEM((2, NBLK), jnp.int32),
            pltpu.SemaphoreType.DMA((len(late),)),
        ],
        compiler_params=LARGE,
    )(c_keep, cols, a_both, part, *late)
    return out.transpose(0, 2, 1, 3)


def per_device(a_vals, a_row, a_col, a_count, b_vals, b_rows, c_keep):
    pa, pb = pack(a_vals, a_row, a_col, a_count, b_vals, b_rows)
    return product(c_keep, spread_a(pa[None]), *spread_b(pb[None]))


def solution(mesh):
    return jax.shard_map(
        per_device,
        mesh=mesh,
        in_specs=(
            P("row", "col", None, None),
            P("row", "col"),
            P("row", "col"),
            P("row", "col"),
            P("row", "col", None, None),
            P("row", "col"),
            P("row", "col"),
        ),
        out_specs=P("row", "col", None, None),
        check_vma=False,
    )
```

```python
import jax
import jax.numpy as jnp
from jax import lax
from jax.experimental import pallas as pl
from jax.experimental.pallas import tpu as pltpu
from jax.sharding import PartitionSpec as P

BLK = 92
LANES = 128
ROWS = 96
HALF = 48
PACKED = ROWS + HALF
REST = LANES - BLK
TAIL = BLK - REST
NOTE = 2 * TAIL
N_Z, N_Y = 16, 8
KA = 16
NBLK = 64
CHUNKS = 32
F32 = jnp.float32
BF16 = jnp.bfloat16
SMEM = pl.BlockSpec(memory_space=pltpu.SMEM)
VMEM = pl.BlockSpec(memory_space=pltpu.VMEM)
LARGE = pltpu.CompilerParams(vmem_limit_bytes=32 * 2**20)
EARLY = pltpu.CompilerParams(vmem_limit_bytes=99 * 2**19)


def lanes_of(shape):
    return lax.broadcasted_iota(jnp.int32, shape, 1)


def pack_into(out_ref, pad, src_ref, notes):
    for s in range(2):
        pad[s, :BLK, :BLK] = src_ref[:, s, :]
    first, second = pad[0], pad[1]
    shifted = pltpu.roll(second, BLK, 1)
    out_ref[:ROWS] = jnp.where(lanes_of((ROWS, LANES)) < BLK, first, shifted)
    low, high = shifted[:HALF], pltpu.roll(shifted[HALF:], TAIL, 1)
    lane = lanes_of((HALF, LANES))
    fold = jnp.where(lane < TAIL, low, high)
    for n, note in enumerate(notes):
        fold = jnp.where(lane == NOTE + n, note.astype(F32), fold)
    out_ref[ROWS:] = fold


def pack_kernel(a_row, a_col, a_count, b_rows, a_ref, b_ref, pa_ref, pb_ref, pad):
    pad[...] = jnp.zeros((2, ROWS, LANES), F32)
    notes = [a_col[0, 0], a_col[0, 1], a_row[0, 0], a_row[0, 1], a_count[0, 0]]
    pack_into(pa_ref, pad, a_ref, notes)
    pack_into(pb_ref, pad, b_ref, [b_rows[0, 0], b_rows[0, 1]])


def first_of(ref, c):
    return jnp.where(lanes_of((ROWS, LANES)) < BLK, ref[c, :ROWS], 0.0)


def second_of(ref, c):
    lane = lanes_of((ROWS, LANES))
    fold = ref[c, ROWS:]
    rest = jnp.concatenate([pltpu.roll(fold, REST, 1), pltpu.roll(fold, LANES - (TAIL - REST), 1)], axis=0)
    return jnp.where(lane < REST, pltpu.roll(ref[c, :ROWS], REST, 1), jnp.where(lane < BLK, rest, 0.0))


def split(x):
    hi = x.astype(BF16)
    return hi, (x - hi.astype(F32)).astype(BF16)


def start_notes(pieces, counts, notes, sems):
    copies, start = [], 0
    for n, (piece, count) in enumerate(zip(pieces, counts)):
        copies.append(pltpu.make_async_copy(piece.at[:, pl.ds(ROWS, 1), :], notes.at[pl.ds(start, count)], sems.at[n]))
        copies[-1].start()
        start += count
    return copies


def padded(x):
    return jnp.concatenate([x, jnp.zeros((LANES - ROWS, LANES), BF16)], axis=0)


def prepare_a(piece, notes, start, a_both, cols, used):
    for i in range(2):
        used[i] = 0

    def listed(c, _):
        live = notes[start + c, 0, NOTE + 4].astype(jnp.int32)
        for s, taken in enumerate((first_of, second_of)):

            @pl.when(s < live)
            def _(s=s, taken=taken):
                i = notes[start + c, 0, NOTE + 2 + s].astype(jnp.int32)
                q = used[i]
                cols[i, q] = notes[start + c, 0, NOTE + s].astype(jnp.int32)
                used[i] = q + 1
                hi, lo = split(taken(piece, c))
                a_both[i, q, :ROWS] = hi
                a_both[i, q, ROWS:] = lo

        return 0

    lax.fori_loop(0, CHUNKS, listed, 0, unroll=8)


def forget(place, zero, unroll):
    def one(n, _):
        place[0, n] = zero
        place[1, n] = zero
        return 0

    lax.fori_loop(0, NBLK, one, 0, unroll=unroll)


def place_b(total, notes, place):
    def one(c, _):
        for j in range(2):
            place[j, notes[c, 0, NOTE + j].astype(jnp.int32)] = 2 * c + j
        return 0

    lax.fori_loop(0, total, one, 0, unroll=4)


def prepare_b(pieces, counts, b_hi, b_lo, place, unroll=8):
    forget(place, 2 * sum(counts), unroll)
    zero = 2 * sum(counts)
    b_hi[zero] = jnp.zeros((LANES, LANES), BF16)
    b_lo[zero] = jnp.zeros((LANES, LANES), BF16)
    start = 0
    for piece, count in zip(pieces, counts):

        def unpack(c, _, piece=piece, start=start):
            n = 2 * (start + c)
            for j, block in enumerate((first_of(piece, c), second_of(piece, c))):
                hi, lo = split(block)
                b_hi[n + j] = padded(hi)
                b_lo[n + j] = padded(lo)
            return 0

        lax.fori_loop(0, count, unpack, 0, unroll=4)
        start += count


def products(i, a_both, cols, b_hi, b_lo, place):
    def pair(p, total):
        both, high = total
        rows_hi, rows_lo = [], []
        for t in range(2):
            k = cols[i, 2 * p + t]
            p0, p1 = place[0, k], place[1, k]
            rows_hi.append(jnp.concatenate([b_hi[p0], b_hi[p1]], axis=1))
            rows_lo.append(jnp.concatenate([b_lo[p0], b_lo[p1]], axis=1))
        a = jnp.concatenate([a_both[i, 2 * p], a_both[i, 2 * p + 1]], axis=1)
        both = both + jnp.dot(a, jnp.concatenate(rows_hi, axis=0), preferred_element_type=F32)
        high = high + jnp.dot(a[:ROWS], jnp.concatenate(rows_lo, axis=0), preferred_element_type=F32)
        return both, high

    zero = (jnp.zeros((2 * ROWS, 2 * LANES), F32), jnp.zeros((ROWS, 2 * LANES), F32))
    both, high = lax.fori_loop(0, KA // 2, pair, zero, unroll=True)
    return both[:ROWS] + both[ROWS:] + high


def early_kernel(counts, a_any, *refs):
    pieces = refs[: len(counts)]
    a_both, cols, part_ref, a_ref, b_hi, b_lo, notes, used, place, sems = refs[len(counts) :]
    a_copy = pltpu.make_async_copy(a_any, a_ref, sems.at[len(counts) + 1])
    copies = start_notes([*pieces, a_any], [*counts, CHUNKS], notes, sems)
    a_copy.start()
    prepare_b(pieces, counts, b_hi, b_lo, place)
    for copy in copies:
        copy.wait()
    place_b(sum(counts), notes, place)
    a_copy.wait()
    prepare_a(a_ref, notes, sum(counts), a_both, cols, used)
    for i in range(2):
        part_ref[i] = products(i, a_both, cols, b_hi, b_lo, place)


def late_kernel(counts, keep, cols, a_both, part_ref, *refs):
    pieces = refs[: len(counts)]
    out_ref, b_hi, b_lo, place = refs[len(counts) :]
    prepare_b(pieces, counts, b_hi, b_lo, place, unroll=True)
    at = 0
    for piece, count in zip(pieces, counts):
        for c in range(count):
            note = piece[c, ROWS : ROWS + 8, :].astype(jnp.int32)
            for j in range(2):
                place[j, note[0, NOTE + j]] = 2 * at + j
            at += 1
    for i in range(2):
        total = part_ref[i] + products(i, a_both, cols, b_hi, b_lo, place)
        for j in range(2):
            kept = keep[i, j].astype(F32)
            out_ref[i, :, j, :] = total[:BLK, j * LANES : j * LANES + BLK] * kept


def pairs(bit):
    return [(n, n ^ bit) for n in range(32)]


def ring_pairs():
    return [(2 * z + h, 2 * ((z + (1 if z % 2 else -1)) % N_Z) + h) for z in range(N_Z) for h in range(2)]


def gather(x, axis, groups):
    return lax.all_gather(x, axis, axis=0, tiled=True, axis_index_groups=groups)


def spread_a(own):
    plane = gather(own, "col", [[4 * y + k for k in range(4)] for y in range(N_Y)])
    return gather(plane, "col", [[4 * y + k for y in range(N_Y)] for k in range(4)])


def spread_b(own):
    move = lambda x, perm: lax.ppermute(x, "row", perm)
    four = gather(own, "row", [[2 * (4 * c + i) + h for c in range(N_Z // 4)] for i in range(4) for h in range(2)])
    second = move(four, pairs(4))
    other = move(four, pairs(1))
    first = move(four, pairs(2))
    third = move(four, ring_pairs())
    late = [move(second, pairs(1)), move(other, ring_pairs())]
    return [four, second, first, third, other, move(other, pairs(2))], late


def pack(a_vals, a_row, a_col, a_count, b_vals, b_rows):
    shape = jax.ShapeDtypeStruct((PACKED, LANES), F32)
    return pl.pallas_call(
        pack_kernel,
        out_shape=(shape, shape),
        in_specs=[SMEM] * 4 + [VMEM] * 2,
        out_specs=(VMEM, VMEM),
        scratch_shapes=[pltpu.VMEM((2, ROWS, LANES), F32)],
    )(a_row, a_col, a_count, b_rows, a_vals[0].transpose(1, 0, 2), b_vals[0].transpose(1, 0, 2))


def scratch(counts):
    blocks = 2 * sum(counts) + 1
    return [pltpu.VMEM((blocks, LANES, LANES), BF16), pltpu.VMEM((blocks, LANES, LANES), BF16)]


def product(c_keep, a_whole, early, late):
    counts = [piece.shape[0] for piece in early]
    a_both, cols, part = pl.pallas_call(
        lambda *refs: early_kernel(counts, *refs),
        out_shape=(
            jax.ShapeDtypeStruct((2, KA, 2 * ROWS, LANES), BF16),
            jax.ShapeDtypeStruct((2, KA), jnp.int32),
            jax.ShapeDtypeStruct((2, ROWS, 2 * LANES), F32),
        ),
        in_specs=[pl.BlockSpec(memory_space=pltpu.HBM)] + [VMEM] * len(early),
        out_specs=(VMEM, SMEM, VMEM),
        scratch_shapes=[
            pltpu.VMEM((CHUNKS, PACKED, LANES), F32),
            *scratch(counts),
            pltpu.SMEM((sum(counts) + CHUNKS, 1, LANES), F32),
            pltpu.SMEM((2,), jnp.int32),
            pltpu.SMEM((2, NBLK), jnp.int32),
            pltpu.SemaphoreType.DMA((len(early) + 2,)),
        ],
        compiler_params=EARLY,
    )(a_whole, *early)
    counts_late = [piece.shape[0] for piece in late]
    out = pl.pallas_call(
        lambda *refs: late_kernel(counts_late, *refs),
        out_shape=jax.ShapeDtypeStruct((2, BLK, 2, BLK), F32),
        in_specs=[SMEM] * 2 + [VMEM] * (2 + len(late)),
        out_specs=VMEM,
        scratch_shapes=[
            *scratch(counts_late),
            pltpu.SMEM((2, NBLK), jnp.int32),
        ],
        compiler_params=LARGE,
    )(c_keep, cols, a_both, part, *late)
    return out.transpose(0, 2, 1, 3)


def per_device(a_vals, a_row, a_col, a_count, b_vals, b_rows, c_keep):
    pa, pb = pack(a_vals, a_row, a_col, a_count, b_vals, b_rows)
    return product(c_keep, spread_a(pa[None]), *spread_b(pb[None]))


def solution(mesh):
    return jax.shard_map(
        per_device,
        mesh=mesh,
        in_specs=(
            P("row", "col", None, None),
            P("row", "col"),
            P("row", "col"),
            P("row", "col"),
            P("row", "col", None, None),
            P("row", "col"),
            P("row", "col"),
        ),
        out_specs=P("row", "col", None, None),
        check_vma=False,
    )
```

```python
import jax
import jax.numpy as jnp
from jax import lax
from jax.experimental import pallas as pl
from jax.experimental.pallas import tpu as pltpu
from jax.sharding import PartitionSpec as P

BLK = 92
LANES = 128
ROWS = 96
HALF = 48
REST = LANES - BLK
TAIL = BLK - REST
PACKED = 136
FOLD = PACKED - HALF
SLIM = LANES - 2 * TAIL
NOTE_ROW, NOTE = 128, 2 * TAIL
N_Z, N_Y = 16, 8
KA = 16
NBLK = 64
CHUNKS = 32
F32 = jnp.float32
BF16 = jnp.bfloat16
SMEM = pl.BlockSpec(memory_space=pltpu.SMEM)
VMEM = pl.BlockSpec(memory_space=pltpu.VMEM)
LARGE = pltpu.CompilerParams(vmem_limit_bytes=32 * 2**20)
EARLY = pltpu.CompilerParams(vmem_limit_bytes=99 * 2**19)


def lanes_of(shape):
    return lax.broadcasted_iota(jnp.int32, shape, 1)


def slim_parts():
    return [(n + 1, SLIM * n) for n in range(4)]


def pack_into(out_ref, pad, src_ref, notes):
    for s in range(2):
        pad[s, :BLK, :BLK] = src_ref[:, s, :]
    first, second = pad[0], pad[1]
    shifted = pltpu.roll(second, BLK, 1)
    main = jnp.where(lanes_of((ROWS, LANES)) < BLK, first, shifted)
    out_ref[:ROWS] = main
    lane = lanes_of((HALF, LANES))
    fold = jnp.where(lane < TAIL, shifted[:HALF], jnp.where(lane < NOTE, pltpu.roll(shifted[HALF:], TAIL, 1), 0.0))
    tiles = [fold[8 * n : 8 * n + 8] for n in range(HALF // 8)]
    lane = lanes_of((8, LANES))
    upper = lax.broadcasted_iota(jnp.int32, (8, LANES), 0) < 4
    tiles[0] = jnp.where(upper, main[ROWS - 8 :], tiles[0])
    turned = pltpu.roll(pltpu.roll(shifted[:8], 4, 0), TAIL, 1)
    tiles[5] = jnp.where(upper | (lane < TAIL) | (lane >= NOTE), tiles[5], turned)
    for tile, begin in slim_parts():
        part = pltpu.roll(shifted[HALF : HALF + 8], NOTE - begin, 1)
        tiles[tile] = jnp.where(upper & (lane >= NOTE), part, tiles[tile])
    for n, note in enumerate(notes):
        tiles[5] = jnp.where(upper & (lane == NOTE + n), note.astype(F32), tiles[5])
    out_ref[FOLD:] = jnp.concatenate(tiles, axis=0)


def pack_kernel(a_row, a_col, a_count, b_rows, a_ref, b_ref, pa_ref, pb_ref, pad):
    pad[...] = jnp.zeros((2, ROWS, LANES), F32)
    notes = [a_col[0, 0], a_col[0, 1], a_row[0, 0], a_row[0, 1], a_count[0, 0]]
    pack_into(pa_ref, pad, a_ref, notes)
    pack_into(pb_ref, pad, b_ref, [b_rows[0, 0], b_rows[0, 1]])


def first_of(ref, c):
    return jnp.where(lanes_of((ROWS, LANES)) < BLK, ref[c, :ROWS], 0.0)


def second_of(ref, c):
    fold = ref[c, FOLD:]
    low, high = pltpu.roll(fold, REST, 1), pltpu.roll(fold, LANES - (TAIL - REST), 1)
    lane = lanes_of((8, LANES))
    upper = lax.broadcasted_iota(jnp.int32, (8, LANES), 0) < 4
    slim = high[:8]
    for tile, begin in slim_parts():
        part = pltpu.roll(fold[8 * tile : 8 * tile + 8], REST + begin + LANES - NOTE, 1)
        slim = jnp.where(upper & (lane >= REST + begin) & (lane < REST + begin + SLIM), part, slim)
    turned = pltpu.roll(high[HALF - 8 :], 4, 0)
    rest = jnp.concatenate([jnp.where(upper, turned, low[:8]), low[8:], slim, high[8:]], axis=0)
    lane = lanes_of((ROWS, LANES))
    return jnp.where(lane < REST, pltpu.roll(ref[c, :ROWS], REST, 1), jnp.where(lane < BLK, rest, 0.0))


def split(x):
    hi = x.astype(BF16)
    return hi, (x - hi.astype(F32)).astype(BF16)


def start_notes(pieces, counts, notes, sems):
    copies, start = [], 0
    for n, (piece, count) in enumerate(zip(pieces, counts)):
        copies.append(pltpu.make_async_copy(piece.at[:, pl.ds(NOTE_ROW, 1), :], notes.at[pl.ds(start, count)], sems.at[n]))
        copies[-1].start()
        start += count
    return copies


def padded(x):
    return jnp.concatenate([x, jnp.zeros((LANES - ROWS, LANES), BF16)], axis=0)


def prepare_a(piece, notes, start, a_both, cols, used):
    for i in range(2):
        used[i] = 0

    def listed(c, _):
        live = notes[start + c, 0, NOTE + 4].astype(jnp.int32)
        for s, taken in enumerate((first_of, second_of)):

            @pl.when(s < live)
            def _(s=s, taken=taken):
                i = notes[start + c, 0, NOTE + 2 + s].astype(jnp.int32)
                q = used[i]
                cols[i, q] = notes[start + c, 0, NOTE + s].astype(jnp.int32)
                used[i] = q + 1
                hi, lo = split(taken(piece, c))
                a_both[i, q, :ROWS] = hi
                a_both[i, q, ROWS:] = lo

        return 0

    lax.fori_loop(0, CHUNKS, listed, 0, unroll=8)


def forget(place, zero, unroll):
    def one(n, _):
        place[0, n] = zero
        place[1, n] = zero
        return 0

    lax.fori_loop(0, NBLK, one, 0, unroll=unroll)


def place_b(total, notes, place):
    def one(c, _):
        for j in range(2):
            place[j, notes[c, 0, NOTE + j].astype(jnp.int32)] = 2 * c + j
        return 0

    lax.fori_loop(0, total, one, 0, unroll=4)


def prepare_b(pieces, counts, b_hi, b_lo, place, unroll=8):
    forget(place, 2 * sum(counts), unroll)
    zero = 2 * sum(counts)
    b_hi[zero] = jnp.zeros((LANES, LANES), BF16)
    b_lo[zero] = jnp.zeros((LANES, LANES), BF16)
    start = 0
    for piece, count in zip(pieces, counts):

        def unpack(c, _, piece=piece, start=start):
            n = 2 * (start + c)
            for j, block in enumerate((first_of(piece, c), second_of(piece, c))):
                hi, lo = split(block)
                b_hi[n + j] = padded(hi)
                b_lo[n + j] = padded(lo)
            return 0

        lax.fori_loop(0, count, unpack, 0, unroll=4)
        start += count


def products(i, a_both, cols, b_hi, b_lo, place):
    def pair(p, total):
        both, high = total
        rows_hi, rows_lo = [], []
        for t in range(2):
            k = cols[i, 2 * p + t]
            p0, p1 = place[0, k], place[1, k]
            rows_hi.append(jnp.concatenate([b_hi[p0], b_hi[p1]], axis=1))
            rows_lo.append(jnp.concatenate([b_lo[p0], b_lo[p1]], axis=1))
        a = jnp.concatenate([a_both[i, 2 * p], a_both[i, 2 * p + 1]], axis=1)
        both = both + jnp.dot(a, jnp.concatenate(rows_hi, axis=0), preferred_element_type=F32)
        high = high + jnp.dot(a[:ROWS], jnp.concatenate(rows_lo, axis=0), preferred_element_type=F32)
        return both, high

    zero = (jnp.zeros((2 * ROWS, 2 * LANES), F32), jnp.zeros((ROWS, 2 * LANES), F32))
    both, high = lax.fori_loop(0, KA // 2, pair, zero, unroll=True)
    return both[:ROWS] + both[ROWS:] + high


def early_kernel(counts, a_any, *refs):
    pieces = refs[: len(counts)]
    a_both, cols, part_ref, a_ref, b_hi, b_lo, notes, used, place, sems = refs[len(counts) :]
    a_copy = pltpu.make_async_copy(a_any, a_ref, sems.at[len(counts) + 1])
    copies = start_notes([*pieces, a_any], [*counts, CHUNKS], notes, sems)
    a_copy.start()
    prepare_b(pieces, counts, b_hi, b_lo, place)
    for copy in copies:
        copy.wait()
    place_b(sum(counts), notes, place)
    a_copy.wait()
    prepare_a(a_ref, notes, sum(counts), a_both, cols, used)
    for i in range(2):
        part_ref[i] = products(i, a_both, cols, b_hi, b_lo, place)


def late_kernel(counts, keep, cols, a_both, part_ref, *refs):
    pieces = refs[: len(counts)]
    out_ref, b_hi, b_lo, place = refs[len(counts) :]
    prepare_b(pieces, counts, b_hi, b_lo, place, unroll=True)
    at = 0
    for piece, count in zip(pieces, counts):
        for c in range(count):
            note = piece[c, NOTE_ROW:, :].astype(jnp.int32)
            for j in range(2):
                place[j, note[0, NOTE + j]] = 2 * at + j
            at += 1
    for i in range(2):
        total = part_ref[i] + products(i, a_both, cols, b_hi, b_lo, place)
        for j in range(2):
            kept = keep[i, j].astype(F32)
            out_ref[i, :, j, :] = total[:BLK, j * LANES : j * LANES + BLK] * kept


def pairs(bit):
    return [(n, n ^ bit) for n in range(32)]


def ring_pairs():
    return [(2 * z + h, 2 * ((z + (1 if z % 2 else -1)) % N_Z) + h) for z in range(N_Z) for h in range(2)]


def gather(x, axis, groups):
    return lax.all_gather(x, axis, axis=0, tiled=True, axis_index_groups=groups)


def spread_a(own):
    plane = gather(own, "col", [[4 * y + k for k in range(4)] for y in range(N_Y)])
    return gather(plane, "col", [[4 * y + k for y in range(N_Y)] for k in range(4)])


def spread_b(own):
    move = lambda x, perm: lax.ppermute(x, "row", perm)
    four = gather(own, "row", [[2 * (4 * c + i) + h for c in range(N_Z // 4)] for i in range(4) for h in range(2)])
    second = move(four, pairs(4))
    other = move(four, pairs(1))
    first = move(four, pairs(2))
    third = move(four, ring_pairs())
    late = [move(second, pairs(1)), move(other, pairs(2)), move(other, ring_pairs())]
    return [four, second, first, third, other], late


def pack(a_vals, a_row, a_col, a_count, b_vals, b_rows):
    shape = jax.ShapeDtypeStruct((PACKED, LANES), F32)
    return pl.pallas_call(
        pack_kernel,
        out_shape=(shape, shape),
        in_specs=[SMEM] * 4 + [VMEM] * 2,
        out_specs=(VMEM, VMEM),
        scratch_shapes=[pltpu.VMEM((2, ROWS, LANES), F32)],
    )(a_row, a_col, a_count, b_rows, a_vals[0].transpose(1, 0, 2), b_vals[0].transpose(1, 0, 2))


def scratch(counts):
    blocks = 2 * sum(counts) + 1
    return [pltpu.VMEM((blocks, LANES, LANES), BF16), pltpu.VMEM((blocks, LANES, LANES), BF16)]


def product(c_keep, a_whole, early, late):
    counts = [piece.shape[0] for piece in early]
    a_both, cols, part = pl.pallas_call(
        lambda *refs: early_kernel(counts, *refs),
        out_shape=(
            jax.ShapeDtypeStruct((2, KA, 2 * ROWS, LANES), BF16),
            jax.ShapeDtypeStruct((2, KA), jnp.int32),
            jax.ShapeDtypeStruct((2, ROWS, 2 * LANES), F32),
        ),
        in_specs=[pl.BlockSpec(memory_space=pltpu.HBM)] + [VMEM] * len(early),
        out_specs=(VMEM, SMEM, VMEM),
        scratch_shapes=[
            pltpu.VMEM((CHUNKS, PACKED, LANES), F32),
            *scratch(counts),
            pltpu.SMEM((sum(counts) + CHUNKS, 1, LANES), F32),
            pltpu.SMEM((2,), jnp.int32),
            pltpu.SMEM((2, NBLK), jnp.int32),
            pltpu.SemaphoreType.DMA((len(early) + 2,)),
        ],
        compiler_params=EARLY,
    )(a_whole, *early)
    counts_late = [piece.shape[0] for piece in late]
    out = pl.pallas_call(
        lambda *refs: late_kernel(counts_late, *refs),
        out_shape=jax.ShapeDtypeStruct((2, BLK, 2, BLK), F32),
        in_specs=[SMEM] * 2 + [VMEM] * (2 + len(late)),
        out_specs=VMEM,
        scratch_shapes=[
            *scratch(counts_late),
            pltpu.SMEM((2, NBLK), jnp.int32),
        ],
        compiler_params=LARGE,
    )(c_keep, cols, a_both, part, *late)
    return out.transpose(0, 2, 1, 3)


def per_device(a_vals, a_row, a_col, a_count, b_vals, b_rows, c_keep):
    pa, pb = pack(a_vals, a_row, a_col, a_count, b_vals, b_rows)
    return product(c_keep, spread_a(pa[None]), *spread_b(pb[None]))


def solution(mesh):
    return jax.shard_map(
        per_device,
        mesh=mesh,
        in_specs=(
            P("row", "col", None, None),
            P("row", "col"),
            P("row", "col"),
            P("row", "col"),
            P("row", "col", None, None),
            P("row", "col"),
            P("row", "col"),
        ),
        out_specs=P("row", "col", None, None),
        check_vma=False,
    )
```

```python
import jax
import jax.numpy as jnp
from jax import lax
from jax.experimental import pallas as pl
from jax.experimental.pallas import tpu as pltpu
from jax.sharding import PartitionSpec as P

BLK = 92
LANES = 128
ROWS = 96
HALF = 48
REST = LANES - BLK
TAIL = BLK - REST
PACKED = 136
FOLD = PACKED - HALF
SLIM = LANES - 2 * TAIL
NOTE_ROW, NOTE = 128, 2 * TAIL
N_Z, N_Y = 16, 8
KA = 16
NBLK = 64
CHUNKS = 32
F32 = jnp.float32
BF16 = jnp.bfloat16
SMEM = pl.BlockSpec(memory_space=pltpu.SMEM)
VMEM = pl.BlockSpec(memory_space=pltpu.VMEM)
LARGE = pltpu.CompilerParams(vmem_limit_bytes=32 * 2**20)
EARLY = pltpu.CompilerParams(vmem_limit_bytes=99 * 2**19)


def lanes_of(shape):
    return lax.broadcasted_iota(jnp.int32, shape, 1)


def slim_parts():
    return [(n + 1, SLIM * n) for n in range(4)]


def pack_into(out_ref, pad, src_ref, notes):
    for s in range(2):
        pad[s, :BLK, :BLK] = src_ref[:, s, :]
    first, second = pad[0], pad[1]
    shifted = pltpu.roll(second, BLK, 1)
    main = jnp.where(lanes_of((ROWS, LANES)) < BLK, first, shifted)
    out_ref[:ROWS] = main
    lane = lanes_of((HALF, LANES))
    fold = jnp.where(lane < TAIL, shifted[:HALF], jnp.where(lane < NOTE, pltpu.roll(shifted[HALF:], TAIL, 1), 0.0))
    tiles = [fold[8 * n : 8 * n + 8] for n in range(HALF // 8)]
    lane = lanes_of((8, LANES))
    upper = lax.broadcasted_iota(jnp.int32, (8, LANES), 0) < 4
    tiles[0] = jnp.where(upper, main[ROWS - 8 :], tiles[0])
    turned = pltpu.roll(pltpu.roll(shifted[:8], 4, 0), TAIL, 1)
    tiles[5] = jnp.where(upper | (lane < TAIL) | (lane >= NOTE), tiles[5], turned)
    for tile, begin in slim_parts():
        part = pltpu.roll(shifted[HALF : HALF + 8], NOTE - begin, 1)
        tiles[tile] = jnp.where(upper & (lane >= NOTE), part, tiles[tile])
    for n, note in enumerate(notes):
        tiles[5] = jnp.where(upper & (lane == NOTE + n), note.astype(F32), tiles[5])
    out_ref[FOLD:] = jnp.concatenate(tiles, axis=0)


def pack_kernel(a_row, a_col, a_count, b_rows, a_ref, b_ref, pa_ref, pb_ref, pad):
    pad[...] = jnp.zeros((2, ROWS, LANES), F32)
    notes = [a_col[0, 0], a_col[0, 1], a_row[0, 0], a_row[0, 1], a_count[0, 0]]
    pack_into(pa_ref, pad, a_ref, notes)
    pack_into(pb_ref, pad, b_ref, [b_rows[0, 0], b_rows[0, 1]])


def first_of(ref, c):
    return jnp.where(lanes_of((ROWS, LANES)) < BLK, ref[c, :ROWS], 0.0)


def second_of(ref, c):
    fold = ref[c, FOLD:]
    low, high = pltpu.roll(fold, REST, 1), pltpu.roll(fold, LANES - (TAIL - REST), 1)
    lane = lanes_of((8, LANES))
    upper = lax.broadcasted_iota(jnp.int32, (8, LANES), 0) < 4
    slim = high[:8]
    for tile, begin in slim_parts():
        part = pltpu.roll(fold[8 * tile : 8 * tile + 8], REST + begin + LANES - NOTE, 1)
        slim = jnp.where(upper & (lane >= REST + begin) & (lane < REST + begin + SLIM), part, slim)
    turned = pltpu.roll(high[HALF - 8 :], 4, 0)
    rest = jnp.concatenate([jnp.where(upper, turned, low[:8]), low[8:], slim, high[8:]], axis=0)
    lane = lanes_of((ROWS, LANES))
    return jnp.where(lane < REST, pltpu.roll(ref[c, :ROWS], REST, 1), jnp.where(lane < BLK, rest, 0.0))


def split(x):
    hi = x.astype(BF16)
    return hi, (x - hi.astype(F32)).astype(BF16)


def start_notes(pieces, counts, notes, sems):
    copies, start = [], 0
    for n, (piece, count) in enumerate(zip(pieces, counts)):
        copies.append(pltpu.make_async_copy(piece.at[:, pl.ds(NOTE_ROW, 1), :], notes.at[pl.ds(start, count)], sems.at[n]))
        copies[-1].start()
        start += count
    return copies


def padded(x):
    return jnp.concatenate([x, jnp.zeros((LANES - ROWS, LANES), BF16)], axis=0)


def prepare_a(piece, notes, start, a_both, cols, used):
    for i in range(2):
        used[i] = 0

    def listed(c, _):
        live = notes[start + c, 0, NOTE + 4].astype(jnp.int32)
        for s, taken in enumerate((first_of, second_of)):

            @pl.when(s < live)
            def _(s=s, taken=taken):
                i = notes[start + c, 0, NOTE + 2 + s].astype(jnp.int32)
                q = used[i]
                cols[i, q] = notes[start + c, 0, NOTE + s].astype(jnp.int32)
                used[i] = q + 1
                hi, lo = split(taken(piece, c))
                a_both[i, q, :ROWS] = hi
                a_both[i, q, ROWS:] = lo

        return 0

    lax.fori_loop(0, CHUNKS, listed, 0, unroll=8)


def forget(place, zero, unroll):
    def one(n, _):
        place[0, n] = zero
        place[1, n] = zero
        return 0

    lax.fori_loop(0, NBLK, one, 0, unroll=unroll)


def place_b(total, notes, place):
    def one(c, _):
        for j in range(2):
            place[j, notes[c, 0, NOTE + j].astype(jnp.int32)] = 2 * c + j
        return 0

    lax.fori_loop(0, total, one, 0, unroll=4)


def prepare_b(pieces, counts, b_hi, b_lo, place, unroll=8):
    forget(place, 2 * sum(counts), unroll)
    zero = 2 * sum(counts)
    b_hi[zero] = jnp.zeros((LANES, LANES), BF16)
    b_lo[zero] = jnp.zeros((LANES, LANES), BF16)
    start = 0
    for piece, count in zip(pieces, counts):

        def unpack(c, _, piece=piece, start=start):
            n = 2 * (start + c)
            for j, block in enumerate((first_of(piece, c), second_of(piece, c))):
                hi, lo = split(block)
                b_hi[n + j] = padded(hi)
                b_lo[n + j] = padded(lo)
            return 0

        lax.fori_loop(0, count, unpack, 0, unroll=4)
        start += count


def products(i, a_both, cols, b_hi, b_lo, place):
    def pair(p, total):
        both, high = total
        rows_hi, rows_lo = [], []
        for t in range(2):
            k = cols[i, 2 * p + t]
            p0, p1 = place[0, k], place[1, k]
            rows_hi.append(jnp.concatenate([b_hi[p0], b_hi[p1]], axis=1))
            rows_lo.append(jnp.concatenate([b_lo[p0], b_lo[p1]], axis=1))
        a = jnp.concatenate([a_both[i, 2 * p], a_both[i, 2 * p + 1]], axis=1)
        both = both + jnp.dot(a, jnp.concatenate(rows_hi, axis=0), preferred_element_type=F32)
        high = high + jnp.dot(a[:ROWS], jnp.concatenate(rows_lo, axis=0), preferred_element_type=F32)
        return both, high

    zero = (jnp.zeros((2 * ROWS, 2 * LANES), F32), jnp.zeros((ROWS, 2 * LANES), F32))
    both, high = lax.fori_loop(0, KA // 2, pair, zero, unroll=True)
    return both[:ROWS] + both[ROWS:] + high


def early_kernel(counts, a_any, *refs):
    pieces = refs[: len(counts)]
    a_both, cols, part_ref, a_ref, b_hi, b_lo, notes, used, place, sems = refs[len(counts) :]
    a_copy = pltpu.make_async_copy(a_any, a_ref, sems.at[len(counts) + 1])
    copies = start_notes([*pieces, a_any], [*counts, CHUNKS], notes, sems)
    a_copy.start()
    prepare_b(pieces, counts, b_hi, b_lo, place)
    for copy in copies:
        copy.wait()
    place_b(sum(counts), notes, place)
    a_copy.wait()
    prepare_a(a_ref, notes, sum(counts), a_both, cols, used)
    for i in range(2):
        part_ref[i] = products(i, a_both, cols, b_hi, b_lo, place)


def late_kernel(counts, keep, cols, a_both, part_ref, *refs):
    pieces = refs[: len(counts)]
    out_ref, b_hi, b_lo, place = refs[len(counts) :]
    prepare_b(pieces, counts, b_hi, b_lo, place, unroll=True)
    at = 0
    for piece, count in zip(pieces, counts):
        for c in range(count):
            note = piece[c, NOTE_ROW:, :].astype(jnp.int32)
            for j in range(2):
                place[j, note[0, NOTE + j]] = 2 * at + j
            at += 1
    for i in range(2):
        total = part_ref[i] + products(i, a_both, cols, b_hi, b_lo, place)
        for j in range(2):
            kept = keep[i, j].astype(F32)
            out_ref[i, :, j, :] = total[:BLK, j * LANES : j * LANES + BLK] * kept


def pairs(bit):
    return [(n, n ^ bit) for n in range(32)]


def ring_pairs():
    return [(2 * z + h, 2 * ((z + (1 if z % 2 else -1)) % N_Z) + h) for z in range(N_Z) for h in range(2)]


def gather(x, axis, groups):
    return lax.all_gather(x, axis, axis=0, tiled=True, axis_index_groups=groups)


def spread_a(own):
    plane = gather(own, "col", [[4 * y + k for k in range(4)] for y in range(N_Y)])
    return gather(plane, "col", [[4 * y + k for y in range(N_Y)] for k in range(4)])


def spread_b(own):
    move = lambda x, perm: lax.ppermute(x, "row", perm)
    four = gather(own, "row", [[2 * (4 * c + i) + h for c in range(N_Z // 4)] for i in range(4) for h in range(2)])
    second = move(four, pairs(4))
    other = move(four, pairs(1))
    first = move(four, pairs(2))
    third = move(four, ring_pairs())
    late = [move(second, pairs(1)), move(other, pairs(2)), move(other, pairs(6))]
    return [four, second, first, third, other], late


def pack(a_vals, a_row, a_col, a_count, b_vals, b_rows):
    shape = jax.ShapeDtypeStruct((PACKED, LANES), F32)
    return pl.pallas_call(
        pack_kernel,
        out_shape=(shape, shape),
        in_specs=[SMEM] * 4 + [VMEM] * 2,
        out_specs=(VMEM, VMEM),
        scratch_shapes=[pltpu.VMEM((2, ROWS, LANES), F32)],
    )(a_row, a_col, a_count, b_rows, a_vals[0].transpose(1, 0, 2), b_vals[0].transpose(1, 0, 2))


def scratch(counts):
    blocks = 2 * sum(counts) + 1
    return [pltpu.VMEM((blocks, LANES, LANES), BF16), pltpu.VMEM((blocks, LANES, LANES), BF16)]


def product(c_keep, a_whole, early, late):
    counts = [piece.shape[0] for piece in early]
    a_both, cols, part = pl.pallas_call(
        lambda *refs: early_kernel(counts, *refs),
        out_shape=(
            jax.ShapeDtypeStruct((2, KA, 2 * ROWS, LANES), BF16),
            jax.ShapeDtypeStruct((2, KA), jnp.int32),
            jax.ShapeDtypeStruct((2, ROWS, 2 * LANES), F32),
        ),
        in_specs=[pl.BlockSpec(memory_space=pltpu.HBM)] + [VMEM] * len(early),
        out_specs=(VMEM, SMEM, VMEM),
        scratch_shapes=[
            pltpu.VMEM((CHUNKS, PACKED, LANES), F32),
            *scratch(counts),
            pltpu.SMEM((sum(counts) + CHUNKS, 1, LANES), F32),
            pltpu.SMEM((2,), jnp.int32),
            pltpu.SMEM((2, NBLK), jnp.int32),
            pltpu.SemaphoreType.DMA((len(early) + 2,)),
        ],
        compiler_params=EARLY,
    )(a_whole, *early)
    counts_late = [piece.shape[0] for piece in late]
    out = pl.pallas_call(
        lambda *refs: late_kernel(counts_late, *refs),
        out_shape=jax.ShapeDtypeStruct((2, BLK, 2, BLK), F32),
        in_specs=[SMEM] * 2 + [VMEM] * (2 + len(late)),
        out_specs=VMEM,
        scratch_shapes=[
            *scratch(counts_late),
            pltpu.SMEM((2, NBLK), jnp.int32),
        ],
        compiler_params=LARGE,
    )(c_keep, cols, a_both, part, *late)
    return out.transpose(0, 2, 1, 3)


def per_device(a_vals, a_row, a_col, a_count, b_vals, b_rows, c_keep):
    pa, pb = pack(a_vals, a_row, a_col, a_count, b_vals, b_rows)
    return product(c_keep, spread_a(pa[None]), *spread_b(pb[None]))


def solution(mesh):
    return jax.shard_map(
        per_device,
        mesh=mesh,
        in_specs=(
            P("row", "col", None, None),
            P("row", "col"),
            P("row", "col"),
            P("row", "col"),
            P("row", "col", None, None),
            P("row", "col"),
            P("row", "col"),
        ),
        out_specs=P("row", "col", None, None),
        check_vma=False,
    )
```
